32 devices in a mesh: tm: 4 (over x, core), space: 8 (over z, y).
Axes of the slice: x: 2, y: 2, z: 4, core: 2. Of those that a mesh axis runs over, the one named last changes fastest.
Arguments:
- vectors: bfloat16 [4, 2, 8, 3, 256, 128], P('tm', None, 'space'), may hold values from -12 to 12
- gauge_links: float32 [4, 3, 2, 8, 3, 3, 128], P('tm', None, None, 'space'), may hold values from -2.5 to 2.5
- perambulator: bfloat16 [4, 64, 2, 256, 256], P('tm', 'space'), may hold values from -0.375 to 0.375
- directions: int32 [4], P('tm'), may hold values from 0 to 2
- momentum: int32 [3], replicated, may hold values from -2 to 2
- source_list: int32 [4], replicated, may hold values from 0 to 3, each once
Outputs:
- elementals: bfloat16 [4, 256, 2, 256], P('tm', 'space')
- correlator: float32 [2, 4, 4], P(None, 'tm')
The draws below stay inside these ranges and needn't reach their ends.
Inputs may be any that keep to these rules, and one draw needn't show every extreme that they name: `directions`: 0, 1, 2 stand for x, y, z. `source_list`: each timeslice is the source of exactly one slot.
All inputs are finite; a program needn't handle non-finite values.
Results may differ from the reference program's by a relative error of at most 0.019.
Values may be sent and summed in bfloat16 or wider, within the bound.
A program may use at most 64 MiB of HBM per device.

```python
import math
import jax
import jax.numpy as jnp
from jax import lax

NV = 256
NS = 4
SX = 16
SY = 8
SMEAR = 2
NT = 4
LZ = 8


def set_ends(values, rng, low, largest):
    index_at = [jax.random.randint(jax.random.fold_in(rng, axis), (), 0, length) for axis, length in enumerate(values.shape)]
    widest = values.shape.index(max(values.shape))
    next_to = index_at[:widest] + [(index_at[widest] + 1) % values.shape[widest]] + index_at[widest + 1:]
    return values.at[tuple(index_at)].set(low).at[tuple(next_to)].set(largest)


def block_scale(stream_key, dims, cuts, smallest, top_value):
    loudness, own = 1.0, jax.random.fold_in(stream_key, 6)
    for dim, shards_of in cuts:
        draws = jnp.exp(jax.random.uniform(jax.random.fold_in(own, dim), (shards_of,), jnp.float32, smallest / len(cuts), top_value / len(cuts)))
        loudness = loudness * jnp.repeat(draws, dims[dim] // shards_of).reshape([-1 if axis == dim else 1 for axis in range(len(dims))])
    return loudness


def scatter_about(rng, dims, deviation, most, pieces=(), kind=jnp.bfloat16):
    entries = deviation * jax.random.normal(rng, dims, jnp.float32)
    if pieces:
        entries = entries * block_scale(rng, dims, pieces, -0.22, 0.18)
    return jnp.clip(entries, -most, most).astype(kind)


def setup_inputs(seed: int = 0) -> dict:
    key_list = jax.random.split(jax.random.key(seed), 7)
    vectors = scatter_about(key_list[0], (NT, 2, LZ, 3, NV, SX * SY), 2.0, 12.0, ((0, 4), (2, 8)))
    gauge_links = scatter_about(key_list[1], (NT, 3, 2, LZ, 3, 3, SX * SY), 0.4, 2.5, ((0, 4), (3, 8)), jnp.float32)
    perambulator = scatter_about(key_list[2], (NT, NT * NS * NS, 2, NV, NV), NV ** -0.5, 0.375, ((0, 4), (1, 8)))
    directions = set_ends(jax.random.randint(key_list[3], (NT,), 0, 3), jax.random.fold_in(key_list[3], 1), 0, 2).astype(jnp.int32)
    momentum = jax.random.randint(key_list[4], (3,), -2, 3).astype(jnp.int32)
    source_list = jax.random.permutation(key_list[5], NT).astype(jnp.int32)
    return dict(vectors=vectors, gauge_links=gauge_links, perambulator=perambulator, directions=directions, momentum=momentum, source_list=source_list)


smear_kappa = 0.05

def colour_apply(link_field, colour_field, adjoint):
    if adjoint:
        link_real = jnp.swapaxes(link_field[0], 1, 2)
        link_imag = -jnp.swapaxes(link_field[1], 1, 2)
    else:
        link_real = link_field[0]
        link_imag = link_field[1]

    def contract(matrix, vector):
        return lax.optimization_barrier(jnp.sum(matrix[:, :, :, None, :] * vector[:, None, :, :, :], axis=2))
    out_real = contract(link_real, colour_field[0]) - contract(link_imag, colour_field[1])
    out_imag = contract(link_real, colour_field[1]) + contract(link_imag, colour_field[0])
    return jnp.stack([out_real, out_imag])

def ahead_x(colour_field):
    column = jnp.arange(colour_field.shape[-1]) % SX
    return jnp.where(column == SX - 1, jnp.roll(colour_field, SX - 1, axis=-1), jnp.roll(colour_field, -1, axis=-1))

def behind_x(colour_field):
    column = jnp.arange(colour_field.shape[-1]) % SX
    return jnp.where(column == 0, jnp.roll(colour_field, 1 - SX, axis=-1), jnp.roll(colour_field, 1, axis=-1))

def rounded_copy(colour_field):
    return lax.optimization_barrier(colour_field.astype(jnp.bfloat16)).astype(jnp.float32)

def smear_once(smeared, link_set):
    colour_field = smeared.astype(jnp.float32)
    summed = -6.0 * colour_field
    for direction in range(3):
        link_field = link_set[direction]
        if direction == 0:
            incoming = ahead_x(colour_field)
        elif direction == 1:
            incoming = jnp.roll(colour_field, -SX, axis=-1)
        else:
            incoming = jnp.roll(colour_field, -1, axis=1)
        carried = colour_apply(link_field, colour_field, True)
        if direction == 0:
            outgoing = behind_x(carried)
        elif direction == 1:
            outgoing = jnp.roll(carried, SX, axis=-1)
        else:
            outgoing = jnp.roll(rounded_copy(carried), 1, axis=1)
        summed = summed + colour_apply(link_field, incoming, False) + outgoing
    return (colour_field + smear_kappa * summed).astype(jnp.bfloat16)

def covariant_step(smeared, link_set, pick):
    colour_field = smeared.astype(jnp.float32)
    link_field = lax.dynamic_index_in_dim(link_set, pick, 0, keepdims=False)
    incoming = jnp.where(pick == 0, ahead_x(colour_field), jnp.where(pick == 1, jnp.roll(colour_field, -SX, axis=-1), jnp.roll(colour_field, -1, axis=1)))
    carried = colour_apply(link_field, colour_field, True)
    outgoing = jnp.where(pick == 0, behind_x(carried), jnp.where(pick == 1, jnp.roll(carried, SX, axis=-1), jnp.roll(rounded_copy(carried), 1, axis=1)))
    return colour_apply(link_field, incoming, False) - outgoing

def phase_angle(momentum, plane_index, extent):
    site_index = jnp.arange(SX * SY)
    column = (site_index % SX).astype(jnp.float32)
    row_index = (site_index // SX).astype(jnp.float32)
    moment = momentum.astype(jnp.float32)
    return 2.0 * math.pi * (moment[0] * column[None, :] / SX + moment[1] * row_index[None, :] / SY + moment[2] * plane_index.astype(jnp.float32)[:, None] / extent)

def project_pair(gradient, angle_grid):
    cosine = jnp.cos(angle_grid)[:, None, None, :]
    sine_part = jnp.sin(angle_grid)[:, None, None, :]
    projected = jnp.stack([cosine * gradient[0] + sine_part * gradient[1], cosine * gradient[1] - sine_part * gradient[0]]).astype(jnp.bfloat16)
    return jnp.stack([projected, jnp.stack([projected[1], -projected[0]])])

def pair_trace(sink, partner, block_set):
    highest = lax.Precision.HIGHEST
    left_side = jnp.stack([jnp.stack([sink[:, 0], -sink[:, 1]], 1), jnp.stack([sink[:, 1], sink[:, 0]], 1)])
    right_side = jnp.stack([jnp.stack([partner[:, 0], partner[:, 1]]), jnp.stack([-partner[:, 1], partner[:, 0]])])
    block_float = block_set.astype(jnp.float32)
    first = jnp.einsum('pirk,brkj->pbij', left_side.astype(jnp.float32), block_float, precision=highest)
    first = rounded_copy(first)
    second = jnp.einsum('pbik,pqkj->qbij', first, right_side.astype(jnp.float32), precision=highest)
    trace_real = jnp.sum(second[0] * block_float[:, 0] + second[1] * block_float[:, 1])
    trace_imag = jnp.sum(second[1] * block_float[:, 0] - second[0] * block_float[:, 1])
    return jnp.stack([trace_real, trace_imag]) / (NS * NV)

def reference(vectors, gauge_links, perambulator, directions, momentum, source_list):
    angle_grid = phase_angle(momentum, jnp.arange(LZ), LZ)
    scale_factor = 1.0 / math.sqrt(3 * SX * SY * LZ)

    def one_slice(inputs):
        smeared, link_set, pick = inputs
        for sweep_index in range(SMEAR):
            smeared = smear_once(smeared, link_set)
        gradient = covariant_step(smeared, link_set, pick)
        paired = project_pair(gradient, angle_grid)
        partial_value = jnp.einsum('rzcas,orzcbs->aob', smeared.astype(jnp.float32), paired.astype(jnp.float32), precision=lax.Precision.HIGHEST)
        return (partial_value * scale_factor).astype(jnp.bfloat16)
    elementals = lax.map(one_slice, (vectors, gauge_links, directions))
    blocks_all = perambulator.reshape(NT, NT, NS * NS, 2, NV, NV)

    def one_sink(inputs):
        sink, sink_blocks = inputs

        def one_pair(pair_inputs):
            block_set, source = pair_inputs
            partner = lax.dynamic_index_in_dim(elementals, source, 0, keepdims=False)
            return pair_trace(sink, partner, block_set)
        return lax.map(one_pair, (sink_blocks, source_list))
    slot_values = lax.map(one_sink, (elementals, blocks_all))
    one_hot = (source_list[:, None] == jnp.arange(NT)[None, :]).astype(jnp.float32)
    correlator = jnp.einsum('tko,ks->ots', slot_values, one_hot, precision=lax.Precision.HIGHEST)
    return (elementals, correlator)
```

```python
import math

import jax
import jax.numpy as jnp
from jax import lax
from jax.experimental import pallas as pl
from jax.experimental.pallas import tpu as pltpu
from jax.sharding import PartitionSpec as P

NS = 4
SX = 16
SY = 8
SMEAR = 2

MESH = pl.DeviceIdType.MESH
smear_kappa = 0.05


def row_chunk(rows):
    return 16 if rows % 16 == 0 else rows


def flat_rows(block):
    count, rows, lanes = block.shape
    if rows % 16 == 0:
        return block.reshape(count * rows, lanes)
    wide = block.astype(jnp.float32).reshape(count * rows, lanes)
    return wide.astype(jnp.bfloat16)


def apply_link(link, field):
    real = []
    imag = []
    for i in range(3):
        total_real = None
        total_imag = None
        for j in range(3):
            link_real, link_imag = link(0, i, j), link(1, i, j)
            term_real = link_real * field[j] - link_imag * field[3 + j]
            term_imag = link_real * field[3 + j] + link_imag * field[j]
            total_real = term_real if j == 0 else total_real + term_real
            total_imag = term_imag if j == 0 else total_imag + term_imag
        real.append(total_real)
        imag.append(total_imag)
    return real + imag


def apply_adjoint(link, field):
    def flipped(part, i, j):
        value = link(part, j, i)
        return value if part == 0 else -value

    real = []
    imag = []
    for i in range(3):
        total_real = None
        total_imag = None
        for j in range(3):
            link_real, link_imag = link(0, j, i), link(1, j, i)
            term_real = link_real * field[j] + link_imag * field[3 + j]
            term_imag = link_real * field[3 + j] - link_imag * field[j]
            total_real = term_real if j == 0 else total_real + term_real
            total_imag = term_imag if j == 0 else total_imag + term_imag
        real.append(total_real)
        imag.append(total_imag)
    return real + imag


def ahead_x(part, column):
    return jnp.where(column == SX - 1, pltpu.roll(part, SX - 1, 1), pltpu.roll(part, SX * SY - 1, 1))


def behind_x(part, column):
    return jnp.where(column == 0, pltpu.roll(part, SX * SY - SX + 1, 1), pltpu.roll(part, 1, 1))


def ahead_y(part):
    return pltpu.roll(part, SX * SY - SX, 1)


def behind_y(part):
    return pltpu.roll(part, SX, 1)


def kernel(
    n,
    nt,
    source_ref,
    field_ref,
    gauge_ref,
    table_ref,
    block_ref,
    own_ref,
    trace_ref,
    gauge_own,
    gauge_send,
    gauge_in,
    gauge_all,
    field_in,
    once,
    twice,
    gradient,
    twice_in,
    gradient_in,
    part_send,
    part_in,
    own_send,
    rows_tm,
    rows_sink,
    source_send,
    rows_source,
    blocks,
    weight,
    trace_send,
    trace_in,
    send_sem,
    recv_sem,
    tm_send_sem,
    tm_recv_sem,
    block_sem,
):
    me = lax.axis_index("space")
    tm_me = lax.axis_index("tm")
    rows = field_ref.shape[2]
    chunk = row_chunk(rows)
    per_plane = rows // chunk
    lanes = SX * SY
    nv = n * rows

    load_blocks = pltpu.make_async_copy(block_ref, blocks, block_sem)
    load_blocks.start()

    barrier = pltpu.get_barrier_semaphore()

    def greet_space(d, carry):
        pl.semaphore_signal(
            barrier, inc=1, device_id={"space": lax.rem(me + d, n)}, device_id_type=MESH
        )
        return carry

    def greet_tm(d, carry):
        pl.semaphore_signal(
            barrier, inc=1, device_id={"tm": lax.rem(tm_me + d, nt)}, device_id_type=MESH
        )
        return carry

    lax.fori_loop(1, n, greet_space, 0)
    lax.fori_loop(1, nt, greet_tm, 0)

    for k in range(gauge_ref.shape[0]):
        gauge_own[pl.ds(3 * k, 3), :] = gauge_ref[k]
    gauge_send[...] = gauge_own[...].astype(jnp.bfloat16)
    gauge_in[me] = gauge_send[...]
    field_in[me] = field_ref[:, me]
    pl.semaphore_wait(barrier, n - 1 + nt - 1)

    def remote(kind, source, target, peer, slot):
        return pltpu.make_async_remote_copy(
            src_ref=source,
            dst_ref=target,
            send_sem=send_sem.at[kind, peer],
            recv_sem=recv_sem.at[kind, slot],
            device_id={"space": peer},
            device_id_type=MESH,
        )

    def each_peer(act):
        def step(d, carry):
            act(lax.rem(me + d, n))
            return carry

        lax.fori_loop(1, n, step, 0)

    def gauge_copy(peer, slot):
        return remote(0, gauge_send, gauge_in.at[slot], peer, slot)

    def field_copy(peer, slot):
        return remote(1, field_ref.at[:, peer], field_in.at[slot], peer, slot)

    def twice_copy(peer, slot):
        return remote(2, twice.at[peer], twice_in.at[slot], peer, slot)

    def gradient_copy(peer, slot):
        return remote(3, gradient.at[peer], gradient_in.at[slot], peer, slot)

    def part_copy(peer, slot):
        return remote(4, part_send.at[peer], part_in.at[slot], peer, slot)

    def sink_copy(peer, slot):
        return remote(5, own_send, rows_sink.at[slot], peer, slot)

    def source_copy(peer, slot):
        return remote(6, source_send.at[peer], rows_source.at[slot], peer, slot)

    def trace_copy(peer, slot):
        return remote(7, trace_send, trace_in.at[slot], peer, slot)

    def start_all(copy):
        each_peer(lambda peer: copy(peer, me).start())

    def arrive_all(copy):
        each_peer(lambda peer: copy(peer, peer).wait_recv())

    start_all(gauge_copy)
    start_all(field_copy)
    arrive_all(gauge_copy)

    def widen(z, carry):
        gauge_all[z] = gauge_in[z].astype(jnp.float32)
        return carry

    lax.fori_loop(0, n, widen, 0)
    arrive_all(field_copy)

    column = lax.broadcasted_iota(jnp.int32, (chunk, lanes), 1) % SX

    def link_at(z, direction):
        def link(part, i, j):
            return gauge_all[z, pl.ds(((direction * 2 + part) * 3 + i) * 3 + j, 1), :]

        return link

    def sweep(held, out, z, piece):
        span = pl.ds(pl.multiple_of(piece * chunk, chunk), chunk)
        above = lax.rem(z + 1, n)
        below = lax.rem(z + n - 1, n)

        def field_at(plane):
            return [held[plane, k, span, :].astype(jnp.float32) for k in range(6)]

        here = field_at(z)
        total = [-6.0 * part for part in here]

        def add(terms):
            for k in range(6):
                total[k] = total[k] + terms[k]

        add(apply_link(link_at(z, 0), [ahead_x(part, column) for part in here]))
        add([behind_x(part, column) for part in apply_adjoint(link_at(z, 0), here)])
        add(apply_link(link_at(z, 1), [ahead_y(part) for part in here]))
        add([behind_y(part) for part in apply_adjoint(link_at(z, 1), here)])
        add(apply_link(link_at(z, 2), field_at(above)))
        add(apply_adjoint(link_at(below, 2), field_at(below)))
        for k in range(6):
            out[z, k, span, :] = (here[k] + smear_kappa * total[k]).astype(jnp.bfloat16)

    def derive(z, piece):
        span = pl.ds(pl.multiple_of(piece * chunk, chunk), chunk)
        above = lax.rem(z + 1, n)
        below = lax.rem(z + n - 1, n)

        def field_at(plane):
            return [twice[plane, k, span, :].astype(jnp.float32) for k in range(6)]

        pick = table_ref[z, pl.ds(2, 1), :]
        along_x = pick == 0.0
        along_y = pick == 1.0
        along_z = pick == 2.0
        wide_x = jnp.broadcast_to(pick, (chunk, lanes)) == 0.0
        wide_y = jnp.broadcast_to(pick, (chunk, lanes)) == 1.0
        wide_z = jnp.broadcast_to(pick, (chunk, lanes)) == 2.0
        links = [link_at(z, direction) for direction in range(3)]
        link_below = link_at(below, 2)

        def chosen(part, i, j):
            return jnp.where(
                along_x,
                links[0](part, i, j),
                jnp.where(along_y, links[1](part, i, j), links[2](part, i, j)),
            )

        def chosen_back(part, i, j):
            return jnp.where(
                along_x,
                links[0](part, i, j),
                jnp.where(along_y, links[1](part, i, j), link_below(part, i, j)),
            )

        here = field_at(z)
        up = field_at(above)
        down = field_at(below)
        incoming = [
            jnp.where(
                wide_x, ahead_x(here[k], column), jnp.where(wide_y, ahead_y(here[k]), up[k])
            )
            for k in range(6)
        ]
        base = [jnp.where(wide_z, down[k], here[k]) for k in range(6)]
        forward = apply_link(chosen, incoming)
        back = apply_adjoint(chosen_back, base)
        back = [
            jnp.where(wide_x, behind_x(part, column), jnp.where(wide_y, behind_y(part), part))
            for part in back
        ]
        slope = [forward[k] - back[k] for k in range(6)]
        cosine = table_ref[z, pl.ds(0, 1), :]
        sine = table_ref[z, pl.ds(1, 1), :]
        for c in range(3):
            real, imag = slope[c], slope[3 + c]
            gradient[z, c, span, :] = (cosine * real + sine * imag).astype(jnp.bfloat16)
            gradient[z, 3 + c, span, :] = (cosine * imag - sine * real).astype(jnp.bfloat16)

    def each_piece(act):
        def step(piece, carry):
            act(piece)
            return carry

        lax.fori_loop(0, per_plane, step, 0)

    bufs = [field_in, once, twice]
    for sweep_index in range(SMEAR - 1):

        def sweep_plane(z, carry):
            each_piece(lambda piece: sweep(bufs[0], bufs[1], z, piece))
            return carry

        lax.fori_loop(0, n, sweep_plane, 0)

    def last_plane(d, carry):
        z = lax.rem(me + d, n)
        each_piece(lambda piece: sweep(once, twice, z, piece))

        @pl.when(d < n)
        def _():
            twice_copy(z, me).start()

        return carry

    lax.fori_loop(1, n + 1, last_plane, 0)
    twice_in[me] = twice[me]

    def derive_plane(d, carry):
        z = lax.rem(me + d, n)
        each_piece(lambda piece: derive(z, piece))

        @pl.when(d < n)
        def _():
            gradient_copy(z, me).start()

        return carry

    lax.fori_loop(1, n + 1, derive_plane, 0)
    gradient_in[me] = gradient[me]

    arrive_all(twice_copy)
    arrive_all(gradient_copy)
    left = jnp.concatenate([flat_rows(twice_in[:, k]) for k in range(6)], axis=1)
    parts = [flat_rows(gradient_in[:, k]) for k in range(6)]
    right_real = jnp.concatenate(parts, axis=1)
    right_imag = jnp.concatenate(parts[3:] + [-part for part in parts[:3]], axis=1)
    nt_dims = (((1,), (1,)), ((), ()))
    sum_real = lax.dot_general(left, right_real, nt_dims, preferred_element_type=jnp.float32)
    sum_imag = lax.dot_general(left, right_imag, nt_dims, preferred_element_type=jnp.float32)
    part_send[:, :, :nv] = sum_real.reshape(n, rows, nv).astype(jnp.bfloat16)
    part_send[:, :, nv:] = sum_imag.reshape(n, rows, nv).astype(jnp.bfloat16)
    part_in[me] = part_send[me]
    start_all(part_copy)
    arrive_all(part_copy)
    scale = 1.0 / math.sqrt(3 * SX * SY * n)
    summed = jnp.sum(part_in[...].astype(jnp.float32), axis=0)
    own = (summed * scale).astype(jnp.bfloat16)
    own_send[...] = own
    own_ref[...] = own
    rows_sink[me] = own
    rows_tm[tm_me] = own

    def tm_copy(peer, slot):
        return pltpu.make_async_remote_copy(
            src_ref=own_send,
            dst_ref=rows_tm.at[slot],
            send_sem=tm_send_sem.at[peer],
            recv_sem=tm_recv_sem.at[slot],
            device_id={"tm": peer},
            device_id_type=MESH,
        )

    def each_tm(act):
        def step(d, carry):
            act(lax.rem(tm_me + d, nt))
            return carry

        lax.fori_loop(1, nt, step, 0)

    each_tm(lambda peer: tm_copy(peer, tm_me).start())
    start_all(sink_copy)
    each_tm(lambda peer: tm_copy(peer, peer).wait_recv())

    def fill_source(i, carry):
        source_send[i] = rows_tm[source_ref[i // (n // nt)]]
        return carry

    lax.fori_loop(0, n, fill_source, 0)
    rows_source[me] = source_send[me]
    start_all(source_copy)
    arrive_all(sink_copy)
    load_blocks.wait()

    sink = flat_rows(rows_sink[...])
    weight[...] = jnp.zeros_like(weight)

    def one_block(q, carry):
        real = blocks[q, 0]
        imag = blocks[q, 1]
        tall = jnp.concatenate([real, -imag], axis=0)
        tall_imag = jnp.concatenate([imag, real], axis=0)
        first_real = jnp.dot(sink, tall, preferred_element_type=jnp.float32)
        first_imag = jnp.dot(sink, tall_imag, preferred_element_type=jnp.float32)
        stacked = jnp.concatenate([first_real, first_imag], axis=0).astype(jnp.bfloat16)
        tn_dims = (((0,), (0,)), ((), ()))
        weight[:, :nv] += lax.dot_general(
            stacked,
            jnp.concatenate([real, imag], axis=0),
            tn_dims,
            preferred_element_type=jnp.float32,
        )
        weight[:, nv:] += lax.dot_general(
            stacked,
            jnp.concatenate([-imag, real], axis=0),
            tn_dims,
            preferred_element_type=jnp.float32,
        )
        return carry

    lax.fori_loop(0, blocks.shape[0], one_block, 0)
    arrive_all(source_copy)
    partner = flat_rows(rows_source[...]).astype(jnp.float32)
    partner_real, partner_imag = partner[:, :nv], partner[:, nv:]
    weight_real, weight_imag = weight[:, :nv], weight[:, nv:]
    trace_real = jnp.sum(partner_real * weight_real - partner_imag * weight_imag)
    trace_imag = jnp.sum(partner_real * weight_imag + partner_imag * weight_real)
    row = lax.broadcasted_iota(jnp.int32, trace_send.shape, 0)
    lane = lax.broadcasted_iota(jnp.int32, trace_send.shape, 1)
    mine = source_ref[me // (n // nt)]
    value = jnp.where(row == 0, trace_real, jnp.where(row == 1, trace_imag, 0.0))
    value = jnp.where(lane == mine, value, 0.0) * (1.0 / (NS * nv))
    trace_send[...] = value
    trace_in[me] = value
    start_all(trace_copy)
    arrive_all(trace_copy)
    trace_ref[...] = jnp.sum(trace_in[...], axis=0)

    for copy in (
        gauge_copy,
        field_copy,
        twice_copy,
        gradient_copy,
        part_copy,
        sink_copy,
        source_copy,
        trace_copy,
    ):
        each_peer(lambda peer: copy(peer, me).wait_send())
    each_tm(lambda peer: tm_copy(peer, tm_me).wait_send())


def per_device(n, nt, vectors, gauge_links, perambulator, directions, momentum, source_list):
    nv = vectors.shape[4]
    lanes = vectors.shape[5]
    rows = nv // n
    field = vectors.reshape(6, n, rows, lanes)
    gauge = gauge_links.reshape(18, 3, lanes)
    block_set = perambulator[0]

    site = jnp.arange(lanes)
    moment = momentum.astype(jnp.float32)
    plane = jnp.arange(n).astype(jnp.float32)
    angle = (
        2.0
        * math.pi
        * (
            moment[0] * (site % SX).astype(jnp.float32)[None, :] / SX
            + moment[1] * (site // SX).astype(jnp.float32)[None, :] / SY
            + moment[2] * plane[:, None] / n
        )
    )
    pick = jnp.broadcast_to(directions[0].astype(jnp.float32), angle.shape)
    table = jnp.stack([jnp.cos(angle), jnp.sin(angle), pick, pick], axis=1)

    bf16, f32 = jnp.bfloat16, jnp.float32
    vmem = pl.BlockSpec(memory_space=pltpu.VMEM)
    smem = pl.BlockSpec(memory_space=pltpu.SMEM)
    anywhere = pl.BlockSpec(memory_space=pl.ANY)
    split = (n, 6, rows, lanes)
    count = block_set.shape[0]
    own, trace = pl.pallas_call(
        lambda *refs: kernel(n, nt, *refs),
        out_shape=(
            jax.ShapeDtypeStruct((rows, 2 * nv), bf16),
            jax.ShapeDtypeStruct((8, 128), f32),
        ),
        in_specs=[smem, vmem, vmem, vmem, anywhere],
        out_specs=(vmem, vmem),
        scratch_shapes=[
            pltpu.VMEM((64, lanes), f32),
            pltpu.VMEM((64, lanes), bf16),
            pltpu.VMEM((n, 64, lanes), bf16),
            pltpu.VMEM((n, 64, lanes), f32),
            pltpu.VMEM(split, bf16),
            pltpu.VMEM(split, bf16),
            pltpu.VMEM(split, bf16),
            pltpu.VMEM(split, bf16),
            pltpu.VMEM(split, bf16),
            pltpu.VMEM(split, bf16),
            pltpu.VMEM((n, rows, 2 * nv), bf16),
            pltpu.VMEM((n, rows, 2 * nv), bf16),
            pltpu.VMEM((rows, 2 * nv), bf16),
            pltpu.VMEM((nt, rows, 2 * nv), bf16),
            pltpu.VMEM((n, rows, 2 * nv), bf16),
            pltpu.VMEM((n, rows, 2 * nv), bf16),
            pltpu.VMEM((n, rows, 2 * nv), bf16),
            pltpu.VMEM((count, 2, nv, nv), bf16),
            pltpu.VMEM((nv, 2 * nv), f32),
            pltpu.VMEM((8, 128), f32),
            pltpu.VMEM((n, 8, 128), f32),
            pltpu.SemaphoreType.DMA((8, n)),
            pltpu.SemaphoreType.DMA((8, n)),
            pltpu.SemaphoreType.DMA((nt,)),
            pltpu.SemaphoreType.DMA((nt,)),
            pltpu.SemaphoreType.DMA,
        ],
        compiler_params=pltpu.CompilerParams(
            collective_id=0, has_side_effects=True, vmem_limit_bytes=40 * 1024 * 1024
        ),
        name="meson",
    )(source_list, field, gauge, table, block_set)
    return (own.reshape(1, rows, 2, nv), trace[:2, None, :nt])


def solution(mesh):
    in_specs = (
        P("tm", None, "space", None, None, None),
        P("tm", None, None, "space", None, None, None),
        P("tm", "space", None, None, None),
        P("tm"),
        P(),
        P(),
    )
    out_specs = (P("tm", "space", None, None), P(None, "tm", None))
    n, nt = mesh.shape["space"], mesh.shape["tm"]

    def body(*args):
        return per_device(n, nt, *args)

    return jax.shard_map(
        body, mesh=mesh, in_specs=in_specs, out_specs=out_specs, check_vma=False
    )
```

```python
import math

import jax
import jax.numpy as jnp
from jax import lax
from jax.experimental import pallas as pl
from jax.experimental.pallas import tpu as pltpu
from jax.sharding import PartitionSpec as P

NS = 4
SX = 16
SY = 8
SMEAR = 2

MESH = pl.DeviceIdType.MESH
smear_kappa = 0.05


def row_chunk(rows):
    return 16 if rows % 16 == 0 else rows


def flat_rows(block):
    count, rows, lanes = block.shape
    if rows % 16 == 0:
        return block.reshape(count * rows, lanes)
    wide = block.astype(jnp.float32).reshape(count * rows, lanes)
    return wide.astype(jnp.bfloat16)


def apply_link(link, field):
    real = []
    imag = []
    for i in range(3):
        total_real = None
        total_imag = None
        for j in range(3):
            link_real, link_imag = link(0, i, j), link(1, i, j)
            term_real = link_real * field[j] - link_imag * field[3 + j]
            term_imag = link_real * field[3 + j] + link_imag * field[j]
            total_real = term_real if j == 0 else total_real + term_real
            total_imag = term_imag if j == 0 else total_imag + term_imag
        real.append(total_real)
        imag.append(total_imag)
    return real + imag


def rounded(field):
    return [part.astype(jnp.bfloat16).astype(jnp.float32) for part in field]


def apply_adjoint(link, field):
    real = []
    imag = []
    for i in range(3):
        total_real = None
        total_imag = None
        for j in range(3):
            link_real, link_imag = link(0, j, i), link(1, j, i)
            term_real = link_real * field[j] + link_imag * field[3 + j]
            term_imag = link_real * field[3 + j] - link_imag * field[j]
            total_real = term_real if j == 0 else total_real + term_real
            total_imag = term_imag if j == 0 else total_imag + term_imag
        real.append(total_real)
        imag.append(total_imag)
    return real + imag


def ahead_x(part, column):
    return jnp.where(column == SX - 1, pltpu.roll(part, SX - 1, 1), pltpu.roll(part, SX * SY - 1, 1))


def behind_x(part, column):
    return jnp.where(column == 0, pltpu.roll(part, SX * SY - SX + 1, 1), pltpu.roll(part, 1, 1))


def ahead_y(part):
    return pltpu.roll(part, SX * SY - SX, 1)


def behind_y(part):
    return pltpu.roll(part, SX, 1)


def kernel(
    n,
    nt,
    source_ref,
    direction_ref,
    momentum_ref,
    field_ref,
    gauge_ref,
    block_ref,
    own_ref,
    trace_ref,
    gauge_own,
    gauge_all,
    table,
    field_in,
    once,
    twice,
    gradient,
    twice_in,
    gradient_in,
    part_send,
    part_in,
    own_send,
    rows_all,
    rows_sink,
    source_send,
    rows_source,
    blocks,
    weight,
    trace_send,
    trace_in,
    send_sem,
    recv_sem,
    tm_send_sem,
    tm_recv_sem,
    block_sem,
    local_sem,
):
    me = lax.axis_index("space")
    tm_me = lax.axis_index("tm")
    per = n // nt
    layer = me // per
    member = tm_me * per + lax.rem(me, per)
    rows = field_ref.shape[2]
    chunk = row_chunk(rows)
    per_plane = rows // chunk
    lanes = SX * SY
    nv = n * rows

    load_blocks = pltpu.make_async_copy(block_ref, blocks, block_sem)
    load_blocks.start()

    def member_id(which, index):
        return {"tm": index // per, "space": which * per + lax.rem(index, per)}

    def each_peer(act, mine=member, lead=1):
        def step(d, carry):
            act(lax.rem(mine + d, n))
            return carry

        lax.fori_loop(lead, n, step, 0)

    def each_layer(act):
        def step(d, carry):
            act(lax.rem(layer + d, nt))
            return carry

        lax.fori_loop(1, nt, step, 0)

    def is_self(device):
        return jnp.logical_and(device["tm"] == tm_me, device["space"] == me)

    barrier = pltpu.get_barrier_semaphore()

    def greet(device):
        pl.semaphore_signal(barrier, inc=1, device_id=device, device_id_type=MESH)

    def greet_origin(plane):
        origin = {"tm": layer, "space": plane}

        @pl.when(jnp.logical_not(is_self(origin)))
        def _():
            greet(origin)

    each_peer(greet_origin, lead=0)
    each_peer(lambda index: greet(member_id(layer, index)))
    each_peer(lambda index: greet({"tm": tm_me, "space": index}), mine=me)
    each_layer(lambda index: greet(member_id(index, member)))

    for k in range(54):
        gauge_own[pl.ds(k, 1), :] = gauge_ref[k]
    towards = direction_ref[0].astype(jnp.float32)
    gauge_own[pl.ds(54, 2), :] = jnp.full((2, lanes), towards, jnp.float32)
    at_home = jnp.where(layer == tm_me, 1, 0)
    pl.semaphore_wait(barrier, n - at_home + n - 1 + n - 1 + nt - 1)

    def remote(kind, source, target, device, peer, slot):
        return pltpu.make_async_remote_copy(
            src_ref=source,
            dst_ref=target,
            send_sem=send_sem.at[kind, peer],
            recv_sem=recv_sem.at[kind, slot],
            device_id=device,
            device_id_type=MESH,
        )

    def gauge_copy(device, peer, slot):
        return remote(0, gauge_own, gauge_all.at[slot], device, peer, slot)

    def field_copy(device, peer, slot):
        return remote(1, field_ref.at[:, peer], field_in.at[slot], device, peer, slot)

    def home_copy():
        return pltpu.make_async_copy(field_ref.at[:, member], field_in.at[me], local_sem)

    def twice_copy(peer, slot):
        return remote(2, twice.at[peer], twice_in.at[slot], member_id(layer, peer), peer, slot)

    def gradient_copy(peer, slot):
        return remote(
            3, gradient.at[peer], gradient_in.at[slot], member_id(layer, peer), peer, slot
        )

    def part_copy(peer, slot):
        return remote(4, part_send.at[peer], part_in.at[slot], member_id(layer, peer), peer, slot)

    def sink_copy(peer, slot):
        return remote(
            5, rows_all.at[peer // per], rows_sink.at[slot], member_id(layer, peer), peer, slot
        )

    def source_copy(peer, slot):
        return remote(6, source_send, rows_source.at[slot], member_id(layer, peer), peer, slot)

    def trace_copy(peer, slot):
        return remote(
            7, trace_send, trace_in.at[slot], {"tm": tm_me, "space": peer}, peer, slot
        )

    def start_all(copy, mine=member):
        each_peer(lambda peer: copy(peer, mine).start(), mine=mine)

    def arrive_all(copy, mine=member):
        each_peer(lambda peer: copy(peer, peer).wait_recv(), mine=mine)

    def send_gauge(peer):
        device = member_id(tm_me, peer)

        @pl.when(jnp.logical_not(is_self(device)))
        def _():
            gauge_copy(device, peer, me).start()

    def send_field(peer):
        device = member_id(tm_me, peer)

        @pl.when(jnp.logical_not(is_self(device)))
        def _():
            field_copy(device, peer, me).start()

    each_peer(send_gauge, lead=0)
    each_peer(send_field, lead=0)

    @pl.when(layer == tm_me)
    def _():
        home_copy().start()
        gauge_all[me] = gauge_own[...]

    plane_at = lax.broadcasted_iota(jnp.int32, (n, lanes), 0).astype(jnp.float32)
    site = lax.broadcasted_iota(jnp.int32, (n, lanes), 1)
    angle = (
        2.0
        * math.pi
        * (
            momentum_ref[0].astype(jnp.float32) * (site % SX).astype(jnp.float32) / SX
            + momentum_ref[1].astype(jnp.float32) * (site // SX).astype(jnp.float32) / SY
            + momentum_ref[2].astype(jnp.float32) * plane_at / n
        )
    )
    table[0] = jnp.cos(angle)
    table[1] = jnp.sin(angle)

    def take_gauge(plane):
        origin = {"tm": layer, "space": plane}

        @pl.when(jnp.logical_not(is_self(origin)))
        def _():
            gauge_copy(member_id(tm_me, lax.rem(member + 1, n)), plane, plane).wait_recv()

    def take_field(plane):
        origin = {"tm": layer, "space": plane}
        mine = is_self(origin)

        @pl.when(jnp.logical_not(mine))
        def _():
            field_copy(member_id(tm_me, lax.rem(member + 1, n)), plane, plane).wait_recv()

        @pl.when(mine)
        def _():
            home_copy().wait()

    each_peer(take_gauge, lead=0)

    column = lax.broadcasted_iota(jnp.int32, (chunk, lanes), 1) % SX

    def link_at(z, direction):
        def link(part, i, j):
            return gauge_all[z, pl.ds(((direction * 2 + part) * 3 + i) * 3 + j, 1), :]

        return link

    def sweep(held, out, z, piece):
        span = pl.ds(pl.multiple_of(piece * chunk, chunk), chunk)
        above = lax.rem(z + 1, n)
        below = lax.rem(z + n - 1, n)

        def field_at(plane):
            return [held[plane, k, span, :].astype(jnp.float32) for k in range(6)]

        here = field_at(z)
        total = [-6.0 * part for part in here]

        def add(terms):
            for k in range(6):
                total[k] = total[k] + terms[k]

        add(apply_link(link_at(z, 0), [ahead_x(part, column) for part in here]))
        add([behind_x(part, column) for part in apply_adjoint(link_at(z, 0), here)])
        add(apply_link(link_at(z, 1), [ahead_y(part) for part in here]))
        add([behind_y(part) for part in apply_adjoint(link_at(z, 1), here)])
        add(apply_link(link_at(z, 2), field_at(above)))
        add(rounded(apply_adjoint(link_at(below, 2), field_at(below))))
        for k in range(6):
            out[z, k, span, :] = (here[k] + smear_kappa * total[k]).astype(jnp.bfloat16)

    def derive(z, piece):
        span = pl.ds(pl.multiple_of(piece * chunk, chunk), chunk)
        above = lax.rem(z + 1, n)
        below = lax.rem(z + n - 1, n)

        def field_at(plane):
            return [twice[plane, k, span, :].astype(jnp.float32) for k in range(6)]

        pick = gauge_all[z, pl.ds(54, 1), :]
        along_x = pick == 0.0
        along_y = pick == 1.0
        along_z = pick == 2.0
        wide_x = jnp.broadcast_to(pick, (chunk, lanes)) == 0.0
        wide_y = jnp.broadcast_to(pick, (chunk, lanes)) == 1.0
        wide_z = jnp.broadcast_to(pick, (chunk, lanes)) == 2.0
        links = [link_at(z, direction) for direction in range(3)]
        link_below = link_at(below, 2)

        def chosen(part, i, j):
            return jnp.where(
                along_x,
                links[0](part, i, j),
                jnp.where(along_y, links[1](part, i, j), links[2](part, i, j)),
            )

        def chosen_back(part, i, j):
            return jnp.where(
                along_x,
                links[0](part, i, j),
                jnp.where(along_y, links[1](part, i, j), link_below(part, i, j)),
            )

        here = field_at(z)
        up = field_at(above)
        down = field_at(below)
        incoming = [
            jnp.where(
                wide_x, ahead_x(here[k], column), jnp.where(wide_y, ahead_y(here[k]), up[k])
            )
            for k in range(6)
        ]
        base = [jnp.where(wide_z, down[k], here[k]) for k in range(6)]
        forward = apply_link(chosen, incoming)
        back = apply_adjoint(chosen_back, base)
        back = [
            jnp.where(wide_x, behind_x(part, column), jnp.where(wide_y, behind_y(part), carried))
            for part, carried in zip(back, rounded(back))
        ]
        slope = [forward[k] - back[k] for k in range(6)]
        cosine = table[0, pl.ds(z, 1), :]
        sine = table[1, pl.ds(z, 1), :]
        for c in range(3):
            real, imag = slope[c], slope[3 + c]
            gradient[z, c, span, :] = (cosine * real + sine * imag).astype(jnp.bfloat16)
            gradient[z, 3 + c, span, :] = (cosine * imag - sine * real).astype(jnp.bfloat16)

    def each_piece(act):
        def step(piece, carry):
            act(piece)
            return carry

        lax.fori_loop(0, per_plane, step, 0)

    turn = jnp.where(2 * layer < nt, 1, -1)
    begin = jnp.where(2 * layer < nt, layer * per + 1, layer * per)

    def first_plane(d, carry):
        z = lax.rem(begin + turn * d + n, n)

        @pl.when(d == 0)
        def _():
            take_field(lax.rem(z - turn + n, n))
            take_field(z)

        @pl.when(d < n - 2)
        def _():
            take_field(lax.rem(z + turn + n, n))

        each_piece(lambda piece: sweep(field_in, once, z, piece))
        return carry

    lax.fori_loop(0, n, first_plane, 0)

    def last_plane(d, carry):
        z = lax.rem(member + d, n)
        each_piece(lambda piece: sweep(once, twice, z, piece))

        @pl.when(d < n)
        def _():
            twice_copy(z, member).start()

        return carry

    lax.fori_loop(1, n + 1, last_plane, 0)
    twice_in[member] = twice[member]

    def derive_plane(d, carry):
        z = lax.rem(member + d, n)
        each_piece(lambda piece: derive(z, piece))

        @pl.when(d < n)
        def _():
            gradient_copy(z, member).start()

        return carry

    lax.fori_loop(1, n + 1, derive_plane, 0)
    gradient_in[member] = gradient[member]

    arrive_all(twice_copy)
    arrive_all(gradient_copy)
    left = jnp.concatenate([flat_rows(twice_in[:, k]) for k in range(6)], axis=1)
    parts = [flat_rows(gradient_in[:, k]) for k in range(6)]
    right_real = jnp.concatenate(parts, axis=1)
    right_imag = jnp.concatenate(parts[3:] + [-part for part in parts[:3]], axis=1)
    nt_dims = (((1,), (1,)), ((), ()))
    sum_real = lax.dot_general(left, right_real, nt_dims, preferred_element_type=jnp.float32)
    sum_imag = lax.dot_general(left, right_imag, nt_dims, preferred_element_type=jnp.float32)
    part_send[:, :, :nv] = sum_real.reshape(n, rows, nv).astype(jnp.bfloat16)
    part_send[:, :, nv:] = sum_imag.reshape(n, rows, nv).astype(jnp.bfloat16)
    part_in[member] = part_send[member]
    start_all(part_copy)
    arrive_all(part_copy)
    scale = 1.0 / math.sqrt(3 * SX * SY * n)
    summed = jnp.sum(part_in[...].astype(jnp.float32), axis=0)
    own = (summed * scale).astype(jnp.bfloat16)
    own_send[...] = own
    rows_all[layer] = own

    def layer_copy(peer, slot):
        return pltpu.make_async_remote_copy(
            src_ref=own_send,
            dst_ref=rows_all.at[slot],
            send_sem=tm_send_sem.at[peer],
            recv_sem=tm_recv_sem.at[slot],
            device_id=member_id(peer, member),
            device_id_type=MESH,
        )

    each_layer(lambda peer: layer_copy(peer, layer).start())
    each_layer(lambda peer: layer_copy(peer, peer).wait_recv())
    start_all(sink_copy)
    source_send[...] = rows_all[source_ref[layer]]
    start_all(source_copy)
    rows_sink[member] = rows_all[tm_me]
    rows_source[member] = source_send[...]
    arrive_all(sink_copy)
    load_blocks.wait()

    mine_rows = rows_sink[me].astype(jnp.float32)
    own_ref[:, 0, :] = mine_rows[:, :nv].astype(jnp.bfloat16)
    own_ref[:, 1, :] = mine_rows[:, nv:].astype(jnp.bfloat16)
    sink = flat_rows(rows_sink[...])
    weight[...] = jnp.zeros_like(weight)

    def one_block(q, carry):
        real = blocks[q, 0]
        imag = blocks[q, 1]
        tall = jnp.concatenate([real, -imag], axis=0)
        tall_imag = jnp.concatenate([imag, real], axis=0)
        first_real = jnp.dot(sink, tall, preferred_element_type=jnp.float32)
        first_imag = jnp.dot(sink, tall_imag, preferred_element_type=jnp.float32)
        stacked = jnp.concatenate([first_real, first_imag], axis=0).astype(jnp.bfloat16)
        tn_dims = (((0,), (0,)), ((), ()))
        weight[:, :nv] += lax.dot_general(
            stacked,
            jnp.concatenate([real, imag], axis=0),
            tn_dims,
            preferred_element_type=jnp.float32,
        )
        weight[:, nv:] += lax.dot_general(
            stacked,
            jnp.concatenate([-imag, real], axis=0),
            tn_dims,
            preferred_element_type=jnp.float32,
        )
        return carry

    lax.fori_loop(0, blocks.shape[0], one_block, 0)
    arrive_all(source_copy)
    partner = flat_rows(rows_source[...]).astype(jnp.float32)
    partner_real, partner_imag = partner[:, :nv], partner[:, nv:]
    weight_real, weight_imag = weight[:, :nv], weight[:, nv:]
    trace_real = jnp.sum(partner_real * weight_real - partner_imag * weight_imag)
    trace_imag = jnp.sum(partner_real * weight_imag + partner_imag * weight_real)
    row = lax.broadcasted_iota(jnp.int32, trace_send.shape, 0)
    lane = lax.broadcasted_iota(jnp.int32, trace_send.shape, 1)
    mine = source_ref[layer]
    value = jnp.where(row == 0, trace_real, jnp.where(row == 1, trace_imag, 0.0))
    value = jnp.where(lane == mine, value, 0.0) * (1.0 / (NS * nv))
    trace_send[...] = value
    trace_in[me] = value
    start_all(trace_copy, mine=me)
    arrive_all(trace_copy, mine=me)
    total = jnp.sum(trace_in[...], axis=0)
    trace_ref[0] = total[0:1, :nt]
    trace_ref[1] = total[1:2, :nt]

    def sent_first(peer):
        device = member_id(tm_me, peer)

        @pl.when(jnp.logical_not(is_self(device)))
        def _():
            gauge_copy(device, peer, me).wait_send()
            field_copy(device, peer, me).wait_send()

    each_peer(sent_first, lead=0)
    for copy in (twice_copy, gradient_copy, part_copy, sink_copy, source_copy):
        each_peer(lambda peer: copy(peer, member).wait_send())
    each_peer(lambda peer: trace_copy(peer, me).wait_send(), mine=me)
    each_layer(lambda peer: layer_copy(peer, layer).wait_send())


def per_device(n, nt, vectors, gauge_links, perambulator, directions, momentum, source_list):
    nv = vectors.shape[4]
    lanes = vectors.shape[5]
    rows = nv // n
    field = vectors.reshape(6, n, rows, lanes)
    gauge = gauge_links.reshape(54, 1, lanes)
    block_set = perambulator[0]

    bf16, f32 = jnp.bfloat16, jnp.float32
    vmem = pl.BlockSpec(memory_space=pltpu.VMEM)
    smem = pl.BlockSpec(memory_space=pltpu.SMEM)
    anywhere = pl.BlockSpec(memory_space=pltpu.HBM)
    split = (n, 6, rows, lanes)
    count = block_set.shape[0]
    own, trace = pl.pallas_call(
        lambda *refs: kernel(n, nt, *refs),
        out_shape=(
            jax.ShapeDtypeStruct((rows, 2, nv), bf16),
            jax.ShapeDtypeStruct((2, 1, nt), f32),
        ),
        in_specs=[smem, smem, smem, anywhere, vmem, anywhere],
        out_specs=(vmem, vmem),
        scratch_shapes=[
            pltpu.VMEM((56, lanes), f32),
            pltpu.VMEM((n, 56, lanes), f32),
            pltpu.VMEM((2, n, lanes), f32),
            pltpu.VMEM(split, bf16),
            pltpu.VMEM(split, bf16),
            pltpu.VMEM(split, bf16),
            pltpu.VMEM(split, bf16),
            pltpu.VMEM(split, bf16),
            pltpu.VMEM(split, bf16),
            pltpu.VMEM((n, rows, 2 * nv), bf16),
            pltpu.VMEM((n, rows, 2 * nv), bf16),
            pltpu.VMEM((rows, 2 * nv), bf16),
            pltpu.VMEM((nt, rows, 2 * nv), bf16),
            pltpu.VMEM((n, rows, 2 * nv), bf16),
            pltpu.VMEM((rows, 2 * nv), bf16),
            pltpu.VMEM((n, rows, 2 * nv), bf16),
            pltpu.VMEM((count, 2, nv, nv), bf16),
            pltpu.VMEM((nv, 2 * nv), f32),
            pltpu.VMEM((8, 128), f32),
            pltpu.VMEM((n, 8, 128), f32),
            pltpu.SemaphoreType.DMA((8, n)),
            pltpu.SemaphoreType.DMA((8, n)),
            pltpu.SemaphoreType.DMA((nt,)),
            pltpu.SemaphoreType.DMA((nt,)),
            pltpu.SemaphoreType.DMA,
            pltpu.SemaphoreType.DMA,
        ],
        compiler_params=pltpu.CompilerParams(
            collective_id=0, has_side_effects=True, vmem_limit_bytes=40 * 1024 * 1024
        ),
        name="meson",
    )(source_list, directions, momentum, field, gauge, block_set)
    return (own[None], trace)


def solution(mesh):
    in_specs = (
        P("tm", None, "space", None, None, None),
        P("tm", None, None, "space", None, None, None),
        P("tm", "space", None, None, None),
        P("tm"),
        P(),
        P(),
    )
    out_specs = (P("tm", "space", None, None), P(None, "tm", None))
    n, nt = mesh.shape["space"], mesh.shape["tm"]

    def body(*args):
        return per_device(n, nt, *args)

    return jax.shard_map(
        body, mesh=mesh, in_specs=in_specs, out_specs=out_specs, check_vma=False
    )
```

```python
import math

import jax
import jax.numpy as jnp
from jax import lax
from jax.experimental import pallas as pl
from jax.experimental.pallas import tpu as pltpu
from jax.sharding import PartitionSpec as P

NS = 4
SX = 16
SY = 8
SMEAR = 2

MESH = pl.DeviceIdType.MESH
smear_kappa = 0.05


def row_chunk(rows):
    return 16 if rows % 16 == 0 else rows


def flat_rows(block):
    count, rows, lanes = block.shape
    if rows % 16 == 0:
        return block.reshape(count * rows, lanes)
    wide = block.astype(jnp.float32).reshape(count * rows, lanes)
    return wide.astype(jnp.bfloat16)


def apply_link(link, field):
    real = []
    imag = []
    for i in range(3):
        total_real = None
        total_imag = None
        for j in range(3):
            link_real, link_imag = link(0, i, j), link(1, i, j)
            term_real = link_real * field[j] - link_imag * field[3 + j]
            term_imag = link_real * field[3 + j] + link_imag * field[j]
            total_real = term_real if j == 0 else total_real + term_real
            total_imag = term_imag if j == 0 else total_imag + term_imag
        real.append(total_real)
        imag.append(total_imag)
    return real + imag


def rounded(field):
    return [part.astype(jnp.bfloat16).astype(jnp.float32) for part in field]


def apply_adjoint(link, field):
    real = []
    imag = []
    for i in range(3):
        total_real = None
        total_imag = None
        for j in range(3):
            link_real, link_imag = link(0, j, i), link(1, j, i)
            term_real = link_real * field[j] + link_imag * field[3 + j]
            term_imag = link_real * field[3 + j] - link_imag * field[j]
            total_real = term_real if j == 0 else total_real + term_real
            total_imag = term_imag if j == 0 else total_imag + term_imag
        real.append(total_real)
        imag.append(total_imag)
    return real + imag


def ahead_x(part, column):
    return jnp.where(column == SX - 1, pltpu.roll(part, SX - 1, 1), pltpu.roll(part, SX * SY - 1, 1))


def behind_x(part, column):
    return jnp.where(column == 0, pltpu.roll(part, SX * SY - SX + 1, 1), pltpu.roll(part, 1, 1))


def ahead_y(part):
    return pltpu.roll(part, SX * SY - SX, 1)


def behind_y(part):
    return pltpu.roll(part, SX, 1)


def kernel(
    n,
    nt,
    source_ref,
    direction_ref,
    momentum_ref,
    field_ref,
    gauge_ref,
    block_ref,
    own_ref,
    trace_ref,
    gauge_own,
    gauge_all,
    gauge_wide,
    table,
    field_in,
    once,
    twice,
    gradient,
    twice_in,
    gradient_in,
    part_send,
    part_in,
    own_send,
    rows_all,
    rows_sink,
    source_send,
    rows_source,
    blocks,
    firsts,
    right_side,
    trace_send,
    trace_in,
    send_sem,
    recv_sem,
    tm_send_sem,
    tm_recv_sem,
    block_sem,
    local_sem,
):
    me = lax.axis_index("space")
    tm_me = lax.axis_index("tm")
    per = n // nt
    layer = me // per
    member = tm_me * per + lax.rem(me, per)
    rows = field_ref.shape[2]
    chunk = row_chunk(rows)
    per_plane = rows // chunk
    lanes = SX * SY
    nv = n * rows

    load_blocks = pltpu.make_async_copy(block_ref, blocks, block_sem)
    load_blocks.start()

    def member_id(which, index):
        return {"tm": index // per, "space": which * per + lax.rem(index, per)}

    def each_peer(act, mine=member, lead=1):
        def step(d, carry):
            act(lax.rem(mine + d, n))
            return carry

        lax.fori_loop(lead, n, step, 0)

    def each_layer(act):
        def step(d, carry):
            act(lax.rem(layer + d, nt))
            return carry

        lax.fori_loop(1, nt, step, 0)

    def is_self(device):
        return jnp.logical_and(device["tm"] == tm_me, device["space"] == me)

    barrier = pltpu.get_barrier_semaphore()

    def greet(device):
        pl.semaphore_signal(barrier, inc=1, device_id=device, device_id_type=MESH)

    def greet_origin(plane):
        origin = {"tm": layer, "space": plane}

        @pl.when(jnp.logical_not(is_self(origin)))
        def _():
            greet(origin)

    def greet_target(index):
        target = member_id(tm_me, index)

        @pl.when(jnp.logical_not(is_self(target)))
        def _():
            greet(target)

    each_peer(greet_origin, lead=0)
    each_peer(greet_target, lead=0)
    each_peer(lambda index: greet(member_id(layer, index)))
    each_peer(lambda index: greet({"tm": tm_me, "space": index}), mine=me)
    each_layer(lambda index: greet(member_id(index, member)))

    for k in range(54):
        gauge_own[k] = gauge_ref[k]
    towards = direction_ref[0].astype(jnp.float32)
    gauge_own[54] = jnp.full((1, lanes), towards, jnp.float32)
    at_home = jnp.where(layer == tm_me, 1, 0)
    pl.semaphore_wait(barrier, 2 * (n - at_home) + n - 1 + n - 1 + nt - 1)

    def remote(kind, source, target, device, peer, slot):
        return pltpu.make_async_remote_copy(
            src_ref=source,
            dst_ref=target,
            send_sem=send_sem.at[kind, peer],
            recv_sem=recv_sem.at[kind, slot],
            device_id=device,
            device_id_type=MESH,
        )

    def gauge_copy(device, peer, slot):
        return remote(0, gauge_own, gauge_all.at[slot], device, peer, slot)

    def field_copy(device, peer, slot):
        return remote(1, field_ref.at[:, peer], field_in.at[slot], device, peer, slot)

    def home_copy():
        return pltpu.make_async_copy(field_ref.at[:, member], field_in.at[me], local_sem)

    def twice_copy(peer, slot):
        return remote(2, twice.at[peer], twice_in.at[slot], member_id(layer, peer), peer, slot)

    def gradient_copy(peer, slot):
        return remote(
            3, gradient.at[peer], gradient_in.at[slot], member_id(layer, peer), peer, slot
        )

    def part_copy(peer, slot):
        return remote(4, part_send.at[peer], part_in.at[slot], member_id(layer, peer), peer, slot)

    def sink_copy(device, peer, slot):
        return remote(5, own_send, rows_sink.at[slot], device, peer, slot)

    def source_copy(peer, slot):
        return remote(6, source_send, rows_source.at[slot], member_id(layer, peer), peer, slot)

    def trace_copy(peer, slot):
        return remote(
            7, trace_send, trace_in.at[slot], {"tm": tm_me, "space": peer}, peer, slot
        )

    def start_all(copy, mine=member):
        each_peer(lambda peer: copy(peer, mine).start(), mine=mine)

    def arrive_all(copy, mine=member):
        each_peer(lambda peer: copy(peer, peer).wait_recv(), mine=mine)

    def send_gauge(peer):
        device = member_id(tm_me, peer)

        @pl.when(jnp.logical_not(is_self(device)))
        def _():
            gauge_copy(device, peer, me).start()

    def send_field(peer):
        device = member_id(tm_me, peer)

        @pl.when(jnp.logical_not(is_self(device)))
        def _():
            field_copy(device, peer, me).start()

    each_peer(send_gauge, lead=0)
    each_peer(send_field, lead=0)

    @pl.when(layer == tm_me)
    def _():
        home_copy().start()
        gauge_all[me] = gauge_own[...]

    plane_at = lax.broadcasted_iota(jnp.int32, (n, lanes), 0).astype(jnp.float32)
    site = lax.broadcasted_iota(jnp.int32, (n, lanes), 1)
    angle = (
        2.0
        * math.pi
        * (
            momentum_ref[0].astype(jnp.float32) * (site % SX).astype(jnp.float32) / SX
            + momentum_ref[1].astype(jnp.float32) * (site // SX).astype(jnp.float32) / SY
            + momentum_ref[2].astype(jnp.float32) * plane_at / n
        )
    )
    table[0] = jnp.cos(angle)
    table[1] = jnp.sin(angle)

    def take_gauge(plane):
        origin = {"tm": layer, "space": plane}

        @pl.when(jnp.logical_not(is_self(origin)))
        def _():
            gauge_copy(member_id(tm_me, lax.rem(member + 1, n)), plane, plane).wait_recv()

    def take_field(plane):
        origin = {"tm": layer, "space": plane}
        mine = is_self(origin)

        @pl.when(jnp.logical_not(mine))
        def _():
            field_copy(member_id(tm_me, lax.rem(member + 1, n)), plane, plane).wait_recv()

        @pl.when(mine)
        def _():
            home_copy().wait()

    each_peer(take_gauge, lead=0)

    def widen(z, carry):
        for k in range(54):
            gauge_wide[z, k] = jnp.broadcast_to(gauge_all[z, k], (8, lanes))
        return carry

    lax.fori_loop(0, n, widen, 0)

    column = lax.broadcasted_iota(jnp.int32, (chunk, lanes), 1) % SX

    def link_at(z, direction):
        def link(part, i, j):
            tile = gauge_wide[z, ((direction * 2 + part) * 3 + i) * 3 + j]
            return jnp.concatenate([tile] * (chunk // 8), axis=0)

        return link

    def sweep(held, out, z, piece):
        span = pl.ds(pl.multiple_of(piece * chunk, chunk), chunk)
        above = lax.rem(z + 1, n)
        below = lax.rem(z + n - 1, n)

        def field_at(plane):
            return [held[plane, k, span, :].astype(jnp.float32) for k in range(6)]

        here = field_at(z)
        total = [-6.0 * part for part in here]

        def add(terms):
            for k in range(6):
                total[k] = total[k] + terms[k]

        add(apply_link(link_at(z, 0), [ahead_x(part, column) for part in here]))
        add([behind_x(part, column) for part in apply_adjoint(link_at(z, 0), here)])
        add(apply_link(link_at(z, 1), [ahead_y(part) for part in here]))
        add([behind_y(part) for part in apply_adjoint(link_at(z, 1), here)])
        add(apply_link(link_at(z, 2), field_at(above)))
        add(rounded(apply_adjoint(link_at(below, 2), field_at(below))))
        for k in range(6):
            out[z, k, span, :] = (here[k] + smear_kappa * total[k]).astype(jnp.bfloat16)

    def derive(z, piece):
        span = pl.ds(pl.multiple_of(piece * chunk, chunk), chunk)
        above = lax.rem(z + 1, n)
        below = lax.rem(z + n - 1, n)

        def field_at(plane):
            return [twice[plane, k, span, :].astype(jnp.float32) for k in range(6)]

        pick = jnp.broadcast_to(gauge_all[z, 54], (chunk, lanes))
        wide_x = pick == 0.0
        wide_y = pick == 1.0
        wide_z = pick == 2.0
        links = [link_at(z, direction) for direction in range(3)]
        link_below = link_at(below, 2)

        def chosen(part, i, j):
            return jnp.where(
                wide_x,
                links[0](part, i, j),
                jnp.where(wide_y, links[1](part, i, j), links[2](part, i, j)),
            )

        def chosen_back(part, i, j):
            return jnp.where(
                wide_x,
                links[0](part, i, j),
                jnp.where(wide_y, links[1](part, i, j), link_below(part, i, j)),
            )

        here = field_at(z)
        up = field_at(above)
        down = field_at(below)
        incoming = [
            jnp.where(
                wide_x, ahead_x(here[k], column), jnp.where(wide_y, ahead_y(here[k]), up[k])
            )
            for k in range(6)
        ]
        base = [jnp.where(wide_z, down[k], here[k]) for k in range(6)]
        forward = apply_link(chosen, incoming)
        back = apply_adjoint(chosen_back, base)
        back = [
            jnp.where(wide_x, behind_x(part, column), jnp.where(wide_y, behind_y(part), carried))
            for part, carried in zip(back, rounded(back))
        ]
        slope = [forward[k] - back[k] for k in range(6)]
        cosine = table[0, pl.ds(z, 1), :]
        sine = table[1, pl.ds(z, 1), :]
        for c in range(3):
            real, imag = slope[c], slope[3 + c]
            gradient[z, c, span, :] = (cosine * real + sine * imag).astype(jnp.bfloat16)
            gradient[z, 3 + c, span, :] = (cosine * imag - sine * real).astype(jnp.bfloat16)

    def each_piece(act):
        def step(piece, carry):
            act(piece)
            return carry

        lax.fori_loop(0, per_plane, step, 0)

    turn = jnp.where(2 * layer < nt, 1, -1)
    begin = jnp.where(2 * layer < nt, layer * per + 1, layer * per)

    def first_plane(d, carry):
        z = lax.rem(begin + turn * d + n, n)

        @pl.when(d == 0)
        def _():
            take_field(lax.rem(z - turn + n, n))
            take_field(z)

        @pl.when(d < n - 2)
        def _():
            take_field(lax.rem(z + turn + n, n))

        each_piece(lambda piece: sweep(field_in, once, z, piece))
        return carry

    lax.fori_loop(0, n, first_plane, 0)

    def last_plane(d, carry):
        z = lax.rem(member + d, n)
        each_piece(lambda piece: sweep(once, twice, z, piece))

        @pl.when(d < n)
        def _():
            twice_copy(z, member).start()

        return carry

    lax.fori_loop(1, n + 1, last_plane, 0)
    twice_in[member] = twice[member]

    def derive_plane(d, carry):
        z = lax.rem(member + d, n)
        each_piece(lambda piece: derive(z, piece))

        @pl.when(d < n)
        def _():
            gradient_copy(z, member).start()

        return carry

    lax.fori_loop(1, n + 1, derive_plane, 0)
    gradient_in[member] = gradient[member]

    arrive_all(twice_copy)
    arrive_all(gradient_copy)
    left = jnp.concatenate([flat_rows(twice_in[:, k]) for k in range(6)], axis=1)
    parts = [flat_rows(gradient_in[:, k]) for k in range(6)]
    right_real = jnp.concatenate(parts, axis=1)
    right_imag = jnp.concatenate(parts[3:] + [-part for part in parts[:3]], axis=1)
    nt_dims = (((1,), (1,)), ((), ()))
    sum_real = lax.dot_general(left, right_real, nt_dims, preferred_element_type=jnp.float32)
    sum_imag = lax.dot_general(left, right_imag, nt_dims, preferred_element_type=jnp.float32)
    part_send[:, :, :nv] = sum_real.reshape(n, rows, nv).astype(jnp.bfloat16)
    part_send[:, :, nv:] = sum_imag.reshape(n, rows, nv).astype(jnp.bfloat16)
    part_in[member] = part_send[member]
    start_all(part_copy)
    arrive_all(part_copy)
    scale = 1.0 / math.sqrt(3 * SX * SY * n)
    summed = jnp.sum(part_in[...].astype(jnp.float32), axis=0)
    own = (summed * scale).astype(jnp.bfloat16)
    own_send[...] = own
    rows_all[layer] = own

    def layer_copy(peer, slot):
        return pltpu.make_async_remote_copy(
            src_ref=own_send,
            dst_ref=rows_all.at[slot],
            send_sem=tm_send_sem.at[peer],
            recv_sem=tm_recv_sem.at[slot],
            device_id=member_id(peer, member),
            device_id_type=MESH,
        )

    def send_sink(plane):
        device = {"tm": layer, "space": plane}

        @pl.when(jnp.logical_not(is_self(device)))
        def _():
            sink_copy(device, plane, member).start()

    def take_sink(index):
        origin = member_id(tm_me, index)

        @pl.when(jnp.logical_not(is_self(origin)))
        def _():
            sink_copy({"tm": tm_me, "space": lax.rem(me + 1, n)}, index, index).wait_recv()

    each_layer(lambda peer: layer_copy(peer, layer).start())
    each_peer(send_sink, mine=me, lead=0)

    @pl.when(layer == tm_me)
    def _():
        rows_sink[member] = own_send[...]

    each_layer(lambda peer: layer_copy(peer, peer).wait_recv())
    source_send[...] = rows_all[source_ref[layer]]
    start_all(source_copy)
    rows_source[member] = source_send[...]
    each_peer(take_sink, lead=0)
    load_blocks.wait()

    mine_rows = rows_sink[me].astype(jnp.float32)
    own_ref[:, 0, :] = mine_rows[:, :nv].astype(jnp.bfloat16)
    own_ref[:, 1, :] = mine_rows[:, nv:].astype(jnp.bfloat16)
    sink = flat_rows(rows_sink[...])

    def first_block(q, carry):
        real = blocks[q, 0]
        imag = blocks[q, 1]
        tall = jnp.concatenate([real, -imag], axis=0)
        tall_imag = jnp.concatenate([imag, real], axis=0)
        firsts[q, :, :nv] = jnp.dot(sink, tall, preferred_element_type=jnp.float32).astype(
            jnp.bfloat16
        )
        firsts[q, :, nv:] = jnp.dot(sink, tall_imag, preferred_element_type=jnp.float32).astype(
            jnp.bfloat16
        )
        return carry

    lax.fori_loop(0, blocks.shape[0], first_block, 0)
    arrive_all(source_copy)
    partner = flat_rows(rows_source[...])
    partner_real, partner_imag = partner[:, :nv], partner[:, nv:]
    right_side[:nv, :nv] = partner_real
    right_side[:nv, nv:] = partner_imag
    right_side[nv:, :nv] = -partner_imag
    right_side[nv:, nv:] = partner_real

    def fold(values):
        return jnp.sum(values.reshape(nv // 8, 8, nv), axis=0)

    def second_block(q, carry):
        sum_real, sum_imag = carry
        second = jnp.dot(firsts[q], right_side[...], preferred_element_type=jnp.float32)
        second_real, second_imag = second[:, :nv], second[:, nv:]
        real = blocks[q, 0].astype(jnp.float32)
        imag = blocks[q, 1].astype(jnp.float32)
        sum_real = sum_real + fold(second_real * real + second_imag * imag)
        sum_imag = sum_imag + fold(second_imag * real - second_real * imag)
        return sum_real, sum_imag

    nothing = jnp.zeros((8, nv), jnp.float32)
    sum_real, sum_imag = lax.fori_loop(0, blocks.shape[0], second_block, (nothing, nothing))
    trace_real = jnp.sum(sum_real)
    trace_imag = jnp.sum(sum_imag)
    row = lax.broadcasted_iota(jnp.int32, trace_send.shape, 0)
    lane = lax.broadcasted_iota(jnp.int32, trace_send.shape, 1)
    mine = source_ref[layer]
    value = jnp.where(row == 0, trace_real, jnp.where(row == 1, trace_imag, 0.0))
    value = jnp.where(lane == mine, value, 0.0) * (1.0 / (NS * nv))
    trace_send[...] = value
    trace_in[me] = value
    start_all(trace_copy, mine=me)
    arrive_all(trace_copy, mine=me)
    total = jnp.sum(trace_in[...], axis=0)
    trace_ref[0] = total[0:1, :nt]
    trace_ref[1] = total[1:2, :nt]

    def sent_first(peer):
        device = member_id(tm_me, peer)

        @pl.when(jnp.logical_not(is_self(device)))
        def _():
            gauge_copy(device, peer, me).wait_send()
            field_copy(device, peer, me).wait_send()

    each_peer(sent_first, lead=0)
    def sent_sink(plane):
        device = {"tm": layer, "space": plane}

        @pl.when(jnp.logical_not(is_self(device)))
        def _():
            sink_copy(device, plane, member).wait_send()

    each_peer(sent_sink, mine=me, lead=0)
    for copy in (twice_copy, gradient_copy, part_copy, source_copy):
        each_peer(lambda peer: copy(peer, member).wait_send())
    each_peer(lambda peer: trace_copy(peer, me).wait_send(), mine=me)
    each_layer(lambda peer: layer_copy(peer, layer).wait_send())


def per_device(n, nt, vectors, gauge_links, perambulator, directions, momentum, source_list):
    nv = vectors.shape[4]
    lanes = vectors.shape[5]
    rows = nv // n
    field = vectors.reshape(6, n, rows, lanes)
    gauge = gauge_links.reshape(54, 1, lanes)
    block_set = perambulator[0]

    bf16, f32 = jnp.bfloat16, jnp.float32
    vmem = pl.BlockSpec(memory_space=pltpu.VMEM)
    smem = pl.BlockSpec(memory_space=pltpu.SMEM)
    anywhere = pl.BlockSpec(memory_space=pltpu.HBM)
    split = (n, 6, rows, lanes)
    count = block_set.shape[0]
    own, trace = pl.pallas_call(
        lambda *refs: kernel(n, nt, *refs),
        out_shape=(
            jax.ShapeDtypeStruct((rows, 2, nv), bf16),
            jax.ShapeDtypeStruct((2, 1, nt), f32),
        ),
        in_specs=[smem, smem, smem, anywhere, vmem, anywhere],
        out_specs=(vmem, vmem),
        scratch_shapes=[
            pltpu.VMEM((55, 1, lanes), f32),
            pltpu.VMEM((n, 55, 1, lanes), f32),
            pltpu.VMEM((n, 54, 8, lanes), f32),
            pltpu.VMEM((2, n, lanes), f32),
            pltpu.VMEM(split, bf16),
            pltpu.VMEM(split, bf16),
            pltpu.VMEM(split, bf16),
            pltpu.VMEM(split, bf16),
            pltpu.VMEM(split, bf16),
            pltpu.VMEM(split, bf16),
            pltpu.VMEM((n, rows, 2 * nv), bf16),
            pltpu.VMEM((n, rows, 2 * nv), bf16),
            pltpu.VMEM((rows, 2 * nv), bf16),
            pltpu.VMEM((nt, rows, 2 * nv), bf16),
            pltpu.VMEM((n, rows, 2 * nv), bf16),
            pltpu.VMEM((rows, 2 * nv), bf16),
            pltpu.VMEM((n, rows, 2 * nv), bf16),
            pltpu.VMEM((count, 2, nv, nv), bf16),
            pltpu.VMEM((count, nv, 2 * nv), bf16),
            pltpu.VMEM((2 * nv, 2 * nv), bf16),
            pltpu.VMEM((8, 128), f32),
            pltpu.VMEM((n, 8, 128), f32),
            pltpu.SemaphoreType.DMA((8, n)),
            pltpu.SemaphoreType.DMA((8, n)),
            pltpu.SemaphoreType.DMA((nt,)),
            pltpu.SemaphoreType.DMA((nt,)),
            pltpu.SemaphoreType.DMA,
            pltpu.SemaphoreType.DMA,
        ],
        compiler_params=pltpu.CompilerParams(
            collective_id=0, has_side_effects=True, vmem_limit_bytes=60 * 1024 * 1024
        ),
        name="meson",
    )(source_list, directions, momentum, field, gauge, block_set)
    return (own[None], trace)


def solution(mesh):
    in_specs = (
        P("tm", None, "space", None, None, None),
        P("tm", None, None, "space", None, None, None),
        P("tm", "space", None, None, None),
        P("tm"),
        P(),
        P(),
    )
    out_specs = (P("tm", "space", None, None), P(None, "tm", None))
    n, nt = mesh.shape["space"], mesh.shape["tm"]

    def body(*args):
        return per_device(n, nt, *args)

    return jax.shard_map(
        body, mesh=mesh, in_specs=in_specs, out_specs=out_specs, check_vma=False
    )
```

```python
import math

import jax
import jax.numpy as jnp
from jax import lax
from jax.experimental import pallas as pl
from jax.experimental.pallas import tpu as pltpu
from jax.sharding import PartitionSpec as P

NS = 4
SX = 16
SY = 8
SMEAR = 2

MESH = pl.DeviceIdType.MESH
smear_kappa = 0.05


def row_chunk(rows):
    return 16 if rows % 16 == 0 else rows


def flat_rows(block):
    count, rows, lanes = block.shape
    if rows % 16 == 0:
        return block.reshape(count * rows, lanes)
    wide = block.astype(jnp.float32).reshape(count * rows, lanes)
    return wide.astype(jnp.bfloat16)


def apply_link(link, field):
    real = []
    imag = []
    for i in range(3):
        total_real = None
        total_imag = None
        for j in range(3):
            link_real, link_imag = link(0, i, j), link(1, i, j)
            term_real = link_real * field[j] - link_imag * field[3 + j]
            term_imag = link_real * field[3 + j] + link_imag * field[j]
            total_real = term_real if j == 0 else total_real + term_real
            total_imag = term_imag if j == 0 else total_imag + term_imag
        real.append(total_real)
        imag.append(total_imag)
    return real + imag


def rounded(field):
    return [part.astype(jnp.bfloat16).astype(jnp.float32) for part in field]


def apply_adjoint(link, field):
    real = []
    imag = []
    for i in range(3):
        total_real = None
        total_imag = None
        for j in range(3):
            link_real, link_imag = link(0, j, i), link(1, j, i)
            term_real = link_real * field[j] + link_imag * field[3 + j]
            term_imag = link_real * field[3 + j] - link_imag * field[j]
            total_real = term_real if j == 0 else total_real + term_real
            total_imag = term_imag if j == 0 else total_imag + term_imag
        real.append(total_real)
        imag.append(total_imag)
    return real + imag


def ahead_x(part, column):
    return jnp.where(column == SX - 1, pltpu.roll(part, SX - 1, 1), pltpu.roll(part, SX * SY - 1, 1))


def behind_x(part, column):
    return jnp.where(column == 0, pltpu.roll(part, SX * SY - SX + 1, 1), pltpu.roll(part, 1, 1))


def ahead_y(part):
    return pltpu.roll(part, SX * SY - SX, 1)


def behind_y(part):
    return pltpu.roll(part, SX, 1)


def kernel(
    n,
    nt,
    source_ref,
    direction_ref,
    momentum_ref,
    field_ref,
    gauge_ref,
    block_ref,
    own_ref,
    trace_ref,
    gauge_own,
    gauge_all,
    gauge_wide,
    table,
    field_in,
    once,
    twice,
    gradient,
    twice_in,
    gradient_in,
    part_send,
    part_in,
    own_send,
    rows_all,
    rows_sink,
    source_send,
    rows_source,
    blocks,
    firsts,
    right_side,
    trace_send,
    trace_in,
    send_sem,
    recv_sem,
    tm_send_sem,
    tm_recv_sem,
    block_sem,
    local_sem,
):
    me = lax.axis_index("space")
    tm_me = lax.axis_index("tm")
    per = n // nt
    layer = me // per
    member = tm_me * per + lax.rem(me, per)
    half = max(nt // 2, 1)

    def layer_of(timeslice):
        return lax.rem(timeslice, 2) * half + timeslice // 2

    def slice_of(index):
        return lax.rem(index, half) * 2 + index // half

    home = layer_of(tm_me)
    held = slice_of(layer)
    rows = field_ref.shape[2]
    chunk = row_chunk(rows)
    per_plane = rows // chunk
    lanes = SX * SY
    nv = n * rows

    load_blocks = pltpu.make_async_copy(block_ref, blocks, block_sem)
    load_blocks.start()

    def member_id(which, index):
        return {"tm": index // per, "space": which * per + lax.rem(index, per)}

    def each_peer(act, mine=member, lead=1):
        def step(d, carry):
            act(lax.rem(mine + d, n))
            return carry

        lax.fori_loop(lead, n, step, 0)

    def each_layer(act):
        def step(d, carry):
            act(lax.rem(layer + d, nt))
            return carry

        lax.fori_loop(1, nt, step, 0)

    def is_self(device):
        return jnp.logical_and(device["tm"] == tm_me, device["space"] == me)

    barrier = pltpu.get_barrier_semaphore()

    def greet(device):
        pl.semaphore_signal(barrier, inc=1, device_id=device, device_id_type=MESH)

    def greet_origin(plane):
        origin = {"tm": held, "space": plane}

        @pl.when(jnp.logical_not(is_self(origin)))
        def _():
            greet(origin)

    def greet_target(index):
        target = member_id(home, index)

        @pl.when(jnp.logical_not(is_self(target)))
        def _():
            greet(target)

    each_peer(greet_origin, lead=0)
    each_peer(greet_target, lead=0)
    each_peer(lambda index: greet(member_id(layer, index)))
    each_peer(lambda index: greet({"tm": tm_me, "space": index}), mine=me)
    each_layer(lambda index: greet(member_id(index, member)))

    for k in range(54):
        gauge_own[k] = gauge_ref[k]
    towards = direction_ref[0].astype(jnp.float32)
    gauge_own[54] = jnp.full((1, lanes), towards, jnp.float32)
    at_home = jnp.where(held == tm_me, 1, 0)
    pl.semaphore_wait(barrier, 2 * (n - at_home) + n - 1 + n - 1 + nt - 1)

    def remote(kind, source, target, device, peer, slot):
        return pltpu.make_async_remote_copy(
            src_ref=source,
            dst_ref=target,
            send_sem=send_sem.at[kind, peer],
            recv_sem=recv_sem.at[kind, slot],
            device_id=device,
            device_id_type=MESH,
        )

    def span_of(piece):
        return pl.ds(pl.multiple_of(piece * chunk, chunk), chunk)

    def gauge_home():
        return remote(1, gauge_own, gauge_all.at[me], member_id(home, me), 0, 0)

    def gauge_copy(peer, slot):
        return remote(
            0, gauge_all.at[slot], gauge_all.at[slot], member_id(layer, peer), peer, slot
        )

    def field_copy(device, peer, slot, piece):
        span = span_of(piece)
        source, target = field_ref.at[:, peer, span], field_in.at[slot, :, span]
        return remote(8 + piece, source, target, device, peer, slot)

    def home_copy(piece):
        span = span_of(piece)
        return pltpu.make_async_copy(
            field_ref.at[:, member, span], field_in.at[me, :, span], local_sem.at[piece]
        )

    def twice_copy(peer, slot, piece):
        span = span_of(piece)
        source, target = twice.at[peer, :, span], twice_in.at[slot, :, span]
        kind = 8 + per_plane + piece
        return remote(kind, source, target, member_id(layer, peer), peer, slot)

    def gradient_copy(peer, slot, piece):
        span = span_of(piece)
        source, target = gradient.at[peer, :, span], gradient_in.at[slot, :, span]
        kind = 8 + 2 * per_plane + piece
        return remote(kind, source, target, member_id(layer, peer), peer, slot)

    def part_copy(peer, slot):
        return remote(4, part_send.at[peer], part_in.at[slot], member_id(layer, peer), peer, slot)

    def sink_copy(device, peer, slot):
        return remote(5, own_send, rows_sink.at[slot], device, peer, slot)

    def source_copy(peer, slot):
        return remote(6, source_send, rows_source.at[slot], member_id(layer, peer), peer, slot)

    def trace_copy(peer, slot):
        return remote(
            7, trace_send, trace_in.at[slot], {"tm": tm_me, "space": peer}, peer, slot
        )

    def start_all(copy, mine=member):
        each_peer(lambda peer: copy(peer, mine).start(), mine=mine)

    def arrive_all(copy, mine=member):
        each_peer(lambda peer: copy(peer, peer).wait_recv(), mine=mine)

    gauge_stays = is_self(member_id(home, me))

    @pl.when(jnp.logical_not(gauge_stays))
    def _():
        gauge_home().start()

    @pl.when(gauge_stays)
    def _():
        gauge_all[me] = gauge_own[...]

    def each_piece(act):
        def step(piece, carry):
            act(piece)
            return carry

        lax.fori_loop(0, per_plane, step, 0)

    def send_fields(piece):
        def send_field(peer):
            device = member_id(home, peer)

            @pl.when(jnp.logical_not(is_self(device)))
            def _():
                field_copy(device, peer, me, piece).start()

        each_peer(send_field, lead=0)

        @pl.when(held == tm_me)
        def _():
            home_copy(piece).start()

    each_piece(send_fields)

    @pl.when(jnp.logical_not(is_self({"tm": held, "space": member})))
    def _():
        gauge_home().wait_recv()

    start_all(gauge_copy)

    plane_at = lax.broadcasted_iota(jnp.int32, (n, lanes), 0).astype(jnp.float32)
    site = lax.broadcasted_iota(jnp.int32, (n, lanes), 1)
    angle = (
        2.0
        * math.pi
        * (
            momentum_ref[0].astype(jnp.float32) * (site % SX).astype(jnp.float32) / SX
            + momentum_ref[1].astype(jnp.float32) * (site // SX).astype(jnp.float32) / SY
            + momentum_ref[2].astype(jnp.float32) * plane_at / n
        )
    )
    table[0] = jnp.cos(angle)
    table[1] = jnp.sin(angle)

    def take_field(plane, piece):
        origin = {"tm": held, "space": plane}
        mine = is_self(origin)

        @pl.when(jnp.logical_not(mine))
        def _():
            device = member_id(home, lax.rem(member + 1, n))
            field_copy(device, plane, plane, piece).wait_recv()

        @pl.when(mine)
        def _():
            home_copy(piece).wait()

    arrive_all(gauge_copy)

    def widen(z, carry):
        for k in range(54):
            gauge_wide[z, k] = jnp.broadcast_to(gauge_all[z, k], (8, lanes))
        return carry

    lax.fori_loop(0, n, widen, 0)

    column = lax.broadcasted_iota(jnp.int32, (chunk, lanes), 1) % SX

    def link_at(z, direction):
        def link(part, i, j):
            tile = gauge_wide[z, ((direction * 2 + part) * 3 + i) * 3 + j]
            return jnp.concatenate([tile] * (chunk // 8), axis=0)

        return link

    def sweep(held, out, z, piece):
        span = pl.ds(pl.multiple_of(piece * chunk, chunk), chunk)
        above = lax.rem(z + 1, n)
        below = lax.rem(z + n - 1, n)

        def field_at(plane):
            return [held[plane, k, span, :].astype(jnp.float32) for k in range(6)]

        here = field_at(z)
        total = [-6.0 * part for part in here]

        def add(terms):
            for k in range(6):
                total[k] = total[k] + terms[k]

        add(apply_link(link_at(z, 0), [ahead_x(part, column) for part in here]))
        add([behind_x(part, column) for part in apply_adjoint(link_at(z, 0), here)])
        add(apply_link(link_at(z, 1), [ahead_y(part) for part in here]))
        add([behind_y(part) for part in apply_adjoint(link_at(z, 1), here)])
        add(apply_link(link_at(z, 2), field_at(above)))
        add(rounded(apply_adjoint(link_at(below, 2), field_at(below))))
        for k in range(6):
            out[z, k, span, :] = (here[k] + smear_kappa * total[k]).astype(jnp.bfloat16)

    def derive(z, piece):
        span = pl.ds(pl.multiple_of(piece * chunk, chunk), chunk)
        above = lax.rem(z + 1, n)
        below = lax.rem(z + n - 1, n)

        def field_at(plane):
            return [twice[plane, k, span, :].astype(jnp.float32) for k in range(6)]

        pick = jnp.broadcast_to(gauge_all[z, 54], (chunk, lanes))
        wide_x = pick == 0.0
        wide_y = pick == 1.0
        wide_z = pick == 2.0
        links = [link_at(z, direction) for direction in range(3)]
        link_below = link_at(below, 2)

        def chosen(part, i, j):
            return jnp.where(
                wide_x,
                links[0](part, i, j),
                jnp.where(wide_y, links[1](part, i, j), links[2](part, i, j)),
            )

        def chosen_back(part, i, j):
            return jnp.where(
                wide_x,
                links[0](part, i, j),
                jnp.where(wide_y, links[1](part, i, j), link_below(part, i, j)),
            )

        here = field_at(z)
        up = field_at(above)
        down = field_at(below)
        incoming = [
            jnp.where(
                wide_x, ahead_x(here[k], column), jnp.where(wide_y, ahead_y(here[k]), up[k])
            )
            for k in range(6)
        ]
        base = [jnp.where(wide_z, down[k], here[k]) for k in range(6)]
        forward = apply_link(chosen, incoming)
        back = apply_adjoint(chosen_back, base)
        back = [
            jnp.where(wide_x, behind_x(part, column), jnp.where(wide_y, behind_y(part), carried))
            for part, carried in zip(back, rounded(back))
        ]
        slope = [forward[k] - back[k] for k in range(6)]
        cosine = table[0, pl.ds(z, 1), :]
        sine = table[1, pl.ds(z, 1), :]
        for c in range(3):
            real, imag = slope[c], slope[3 + c]
            gradient[z, c, span, :] = (cosine * real + sine * imag).astype(jnp.bfloat16)
            gradient[z, 3 + c, span, :] = (cosine * imag - sine * real).astype(jnp.bfloat16)

    turn = jnp.where(2 * layer < nt, 1, -1)
    begin = jnp.where(2 * layer < nt, layer * per + 1, layer * per)

    def work(piece):
        def first_plane(d, carry):
            z = lax.rem(begin + turn * d + n, n)

            @pl.when(d == 0)
            def _():
                take_field(lax.rem(z - turn + n, n), piece)
                take_field(z, piece)

            @pl.when(d < n - 2)
            def _():
                take_field(lax.rem(z + turn + n, n), piece)

            sweep(field_in, once, z, piece)
            return carry

        def last_plane(d, carry):
            z = lax.rem(member + d, n)
            sweep(once, twice, z, piece)

            @pl.when(d < n)
            def _():
                twice_copy(z, member, piece).start()

            return carry

        def derive_plane(d, carry):
            z = lax.rem(member + d, n)
            derive(z, piece)

            @pl.when(d < n)
            def _():
                gradient_copy(z, member, piece).start()

            return carry

        lax.fori_loop(0, n, first_plane, 0)
        lax.fori_loop(1, n + 1, last_plane, 0)
        lax.fori_loop(1, n + 1, derive_plane, 0)

    each_piece(work)
    twice_in[member] = twice[member]
    gradient_in[member] = gradient[member]

    def arrive_piece(piece):
        each_peer(lambda peer: twice_copy(peer, peer, piece).wait_recv())
        each_peer(lambda peer: gradient_copy(peer, peer, piece).wait_recv())

    each_piece(arrive_piece)
    left = jnp.concatenate([flat_rows(twice_in[:, k]) for k in range(6)], axis=1)
    parts = [flat_rows(gradient_in[:, k]) for k in range(6)]
    right_real = jnp.concatenate(parts, axis=1)
    right_imag = jnp.concatenate(parts[3:] + [-part for part in parts[:3]], axis=1)
    nt_dims = (((1,), (1,)), ((), ()))
    sum_real = lax.dot_general(left, right_real, nt_dims, preferred_element_type=jnp.float32)
    sum_imag = lax.dot_general(left, right_imag, nt_dims, preferred_element_type=jnp.float32)
    part_send[:, :, :nv] = sum_real.reshape(n, rows, nv).astype(jnp.bfloat16)
    part_send[:, :, nv:] = sum_imag.reshape(n, rows, nv).astype(jnp.bfloat16)
    part_in[member] = part_send[member]
    start_all(part_copy)
    arrive_all(part_copy)
    scale = 1.0 / math.sqrt(3 * SX * SY * n)
    summed = jnp.sum(part_in[...].astype(jnp.float32), axis=0)
    own = (summed * scale).astype(jnp.bfloat16)
    own_send[...] = own
    rows_all[held] = own

    def layer_copy(peer, slot):
        return pltpu.make_async_remote_copy(
            src_ref=own_send,
            dst_ref=rows_all.at[slot],
            send_sem=tm_send_sem.at[peer],
            recv_sem=tm_recv_sem.at[slot],
            device_id=member_id(peer, member),
            device_id_type=MESH,
        )

    def send_sink(plane):
        device = {"tm": held, "space": plane}

        @pl.when(jnp.logical_not(is_self(device)))
        def _():
            sink_copy(device, plane, member).start()

    def take_sink(index):
        origin = member_id(home, index)

        @pl.when(jnp.logical_not(is_self(origin)))
        def _():
            sink_copy({"tm": tm_me, "space": lax.rem(me + 1, n)}, index, index).wait_recv()

    each_layer(lambda peer: layer_copy(peer, held).start())
    each_peer(send_sink, mine=me, lead=0)

    @pl.when(held == tm_me)
    def _():
        rows_sink[member] = own_send[...]

    each_layer(lambda peer: layer_copy(peer, slice_of(peer)).wait_recv())
    source_send[...] = rows_all[source_ref[layer]]
    start_all(source_copy)
    rows_source[member] = source_send[...]
    each_peer(take_sink, lead=0)
    load_blocks.wait()

    mine_rows = rows_sink[me].astype(jnp.float32)
    own_ref[:, 0, :] = mine_rows[:, :nv].astype(jnp.bfloat16)
    own_ref[:, 1, :] = mine_rows[:, nv:].astype(jnp.bfloat16)
    sink = flat_rows(rows_sink[...])

    def first_block(q, carry):
        real = blocks[q, 0]
        imag = blocks[q, 1]
        tall = jnp.concatenate([real, -imag], axis=0)
        tall_imag = jnp.concatenate([imag, real], axis=0)
        firsts[q, :, :nv] = jnp.dot(sink, tall, preferred_element_type=jnp.float32).astype(
            jnp.bfloat16
        )
        firsts[q, :, nv:] = jnp.dot(sink, tall_imag, preferred_element_type=jnp.float32).astype(
            jnp.bfloat16
        )
        return carry

    lax.fori_loop(0, blocks.shape[0], first_block, 0)
    arrive_all(source_copy)
    partner = flat_rows(rows_source[...])
    partner_real, partner_imag = partner[:, :nv], partner[:, nv:]
    right_side[:nv, :nv] = partner_real
    right_side[:nv, nv:] = partner_imag
    right_side[nv:, :nv] = -partner_imag
    right_side[nv:, nv:] = partner_real

    def fold(values):
        return jnp.sum(values.reshape(nv // 8, 8, nv), axis=0)

    def second_block(q, carry):
        sum_real, sum_imag = carry
        second = jnp.dot(firsts[q], right_side[...], preferred_element_type=jnp.float32)
        second_real, second_imag = second[:, :nv], second[:, nv:]
        real = blocks[q, 0].astype(jnp.float32)
        imag = blocks[q, 1].astype(jnp.float32)
        sum_real = sum_real + fold(second_real * real + second_imag * imag)
        sum_imag = sum_imag + fold(second_imag * real - second_real * imag)
        return sum_real, sum_imag

    nothing = jnp.zeros((8, nv), jnp.float32)
    sum_real, sum_imag = lax.fori_loop(0, blocks.shape[0], second_block, (nothing, nothing))
    trace_real = jnp.sum(sum_real)
    trace_imag = jnp.sum(sum_imag)
    row = lax.broadcasted_iota(jnp.int32, trace_send.shape, 0)
    lane = lax.broadcasted_iota(jnp.int32, trace_send.shape, 1)
    mine = source_ref[layer]
    value = jnp.where(row == 0, trace_real, jnp.where(row == 1, trace_imag, 0.0))
    value = jnp.where(lane == mine, value, 0.0) * (1.0 / (NS * nv))
    trace_send[...] = value
    trace_in[me] = value
    start_all(trace_copy, mine=me)
    arrive_all(trace_copy, mine=me)
    total = jnp.sum(trace_in[...], axis=0)
    trace_ref[0] = total[0:1, :nt]
    trace_ref[1] = total[1:2, :nt]

    @pl.when(jnp.logical_not(gauge_stays))
    def _():
        gauge_home().wait_send()

    def sent_piece(piece):
        def sent_field(peer):
            device = member_id(home, peer)

            @pl.when(jnp.logical_not(is_self(device)))
            def _():
                field_copy(device, peer, me, piece).wait_send()

        each_peer(sent_field, lead=0)
        each_peer(lambda peer: twice_copy(peer, member, piece).wait_send())
        each_peer(lambda peer: gradient_copy(peer, member, piece).wait_send())

    each_piece(sent_piece)

    def sent_sink(plane):
        device = {"tm": held, "space": plane}

        @pl.when(jnp.logical_not(is_self(device)))
        def _():
            sink_copy(device, plane, member).wait_send()

    each_peer(sent_sink, mine=me, lead=0)
    for copy in (gauge_copy, part_copy, source_copy):
        each_peer(lambda peer: copy(peer, member).wait_send())
    each_peer(lambda peer: trace_copy(peer, me).wait_send(), mine=me)
    each_layer(lambda peer: layer_copy(peer, held).wait_send())


def per_device(n, nt, vectors, gauge_links, perambulator, directions, momentum, source_list):
    nv = vectors.shape[4]
    lanes = vectors.shape[5]
    rows = nv // n
    field = vectors.reshape(6, n, rows, lanes)
    gauge = gauge_links.reshape(54, 1, lanes)
    block_set = perambulator[0]

    bf16, f32 = jnp.bfloat16, jnp.float32
    vmem = pl.BlockSpec(memory_space=pltpu.VMEM)
    smem = pl.BlockSpec(memory_space=pltpu.SMEM)
    anywhere = pl.BlockSpec(memory_space=pltpu.HBM)
    split = (n, 6, rows, lanes)
    count = block_set.shape[0]
    pieces = rows // row_chunk(rows)
    own, trace = pl.pallas_call(
        lambda *refs: kernel(n, nt, *refs),
        out_shape=(
            jax.ShapeDtypeStruct((rows, 2, nv), bf16),
            jax.ShapeDtypeStruct((2, 1, nt), f32),
        ),
        in_specs=[smem, smem, smem, anywhere, vmem, anywhere],
        out_specs=(vmem, vmem),
        scratch_shapes=[
            pltpu.VMEM((55, 1, lanes), f32),
            pltpu.VMEM((n, 55, 1, lanes), f32),
            pltpu.VMEM((n, 54, 8, lanes), f32),
            pltpu.VMEM((2, n, lanes), f32),
            pltpu.VMEM(split, bf16),
            pltpu.VMEM(split, bf16),
            pltpu.VMEM(split, bf16),
            pltpu.VMEM(split, bf16),
            pltpu.VMEM(split, bf16),
            pltpu.VMEM(split, bf16),
            pltpu.VMEM((n, rows, 2 * nv), bf16),
            pltpu.VMEM((n, rows, 2 * nv), bf16),
            pltpu.VMEM((rows, 2 * nv), bf16),
            pltpu.VMEM((nt, rows, 2 * nv), bf16),
            pltpu.VMEM((n, rows, 2 * nv), bf16),
            pltpu.VMEM((rows, 2 * nv), bf16),
            pltpu.VMEM((n, rows, 2 * nv), bf16),
            pltpu.VMEM((count, 2, nv, nv), bf16),
            pltpu.VMEM((count, nv, 2 * nv), bf16),
            pltpu.VMEM((2 * nv, 2 * nv), bf16),
            pltpu.VMEM((8, 128), f32),
            pltpu.VMEM((n, 8, 128), f32),
            pltpu.SemaphoreType.DMA((8 + 3 * pieces, n)),
            pltpu.SemaphoreType.DMA((8 + 3 * pieces, n)),
            pltpu.SemaphoreType.DMA((nt,)),
            pltpu.SemaphoreType.DMA((nt,)),
            pltpu.SemaphoreType.DMA,
            pltpu.SemaphoreType.DMA((pieces,)),
        ],
        compiler_params=pltpu.CompilerParams(
            collective_id=0, has_side_effects=True, vmem_limit_bytes=60 * 1024 * 1024
        ),
        name="meson",
    )(source_list, directions, momentum, field, gauge, block_set)
    return (own[None], trace)


def solution(mesh):
    in_specs = (
        P("tm", None, "space", None, None, None),
        P("tm", None, None, "space", None, None, None),
        P("tm", "space", None, None, None),
        P("tm"),
        P(),
        P(),
    )
    out_specs = (P("tm", "space", None, None), P(None, "tm", None))
    n, nt = mesh.shape["space"], mesh.shape["tm"]

    def body(*args):
        return per_device(n, nt, *args)

    return jax.shard_map(
        body, mesh=mesh, in_specs=in_specs, out_specs=out_specs, check_vma=False
    )
```

```python
import math

import jax
import jax.numpy as jnp
from jax import lax
from jax.experimental import pallas as pl
from jax.experimental.pallas import tpu as pltpu
from jax.sharding import PartitionSpec as P

NS = 4
SX = 16
SY = 8
SMEAR = 2

MESH = pl.DeviceIdType.MESH
smear_kappa = 0.05


def row_chunk(rows):
    return 16 if rows % 16 == 0 else rows


def flat_rows(block):
    count, rows, lanes = block.shape
    if rows % 16 == 0:
        return block.reshape(count * rows, lanes)
    wide = block.astype(jnp.float32).reshape(count * rows, lanes)
    return wide.astype(jnp.bfloat16)


def apply_link(link, field):
    real = []
    imag = []
    for i in range(3):
        total_real = None
        total_imag = None
        for j in range(3):
            link_real, link_imag = link(0, i, j), link(1, i, j)
            term_real = link_real * field[j] - link_imag * field[3 + j]
            term_imag = link_real * field[3 + j] + link_imag * field[j]
            total_real = term_real if j == 0 else total_real + term_real
            total_imag = term_imag if j == 0 else total_imag + term_imag
        real.append(total_real)
        imag.append(total_imag)
    return real + imag


def rounded(field):
    return [part.astype(jnp.bfloat16).astype(jnp.float32) for part in field]


def apply_adjoint(link, field):
    real = []
    imag = []
    for i in range(3):
        total_real = None
        total_imag = None
        for j in range(3):
            link_real, link_imag = link(0, j, i), link(1, j, i)
            term_real = link_real * field[j] + link_imag * field[3 + j]
            term_imag = link_real * field[3 + j] - link_imag * field[j]
            total_real = term_real if j == 0 else total_real + term_real
            total_imag = term_imag if j == 0 else total_imag + term_imag
        real.append(total_real)
        imag.append(total_imag)
    return real + imag


def ahead_x(part, column):
    return jnp.where(column == SX - 1, pltpu.roll(part, SX - 1, 1), pltpu.roll(part, SX * SY - 1, 1))


def behind_x(part, column):
    return jnp.where(column == 0, pltpu.roll(part, SX * SY - SX + 1, 1), pltpu.roll(part, 1, 1))


def ahead_y(part):
    return pltpu.roll(part, SX * SY - SX, 1)


def behind_y(part):
    return pltpu.roll(part, SX, 1)


def kernel(
    n,
    nt,
    source_ref,
    direction_ref,
    momentum_ref,
    field_ref,
    gauge_ref,
    block_ref,
    own_ref,
    trace_ref,
    gauge_own,
    gauge_all,
    gauge_wide,
    table,
    field_in,
    once,
    twice,
    gradient,
    twice_in,
    gradient_in,
    part_send,
    part_in,
    own_send,
    rows_all,
    rows_sink,
    source_send,
    rows_source,
    blocks,
    firsts,
    right_side,
    trace_send,
    trace_in,
    send_sem,
    recv_sem,
    tm_send_sem,
    tm_recv_sem,
    block_sem,
    local_sem,
):
    me = lax.axis_index("space")
    tm_me = lax.axis_index("tm")
    per = n // nt
    layer = me // per
    member = tm_me * per + lax.rem(me, per)
    half = max(nt // 2, 1)

    def layer_of(timeslice):
        return lax.rem(timeslice, 2) * half + timeslice // 2

    def slice_of(index):
        return lax.rem(index, half) * 2 + index // half

    home = layer_of(tm_me)
    held = slice_of(layer)
    rows = field_ref.shape[2]
    chunk = row_chunk(rows)
    per_plane = rows // chunk
    lanes = SX * SY
    nv = n * rows

    load_blocks = pltpu.make_async_copy(block_ref, blocks, block_sem)
    load_blocks.start()

    def member_id(which, index):
        return {"tm": index // per, "space": which * per + lax.rem(index, per)}

    def each_peer(act, mine=member, lead=1):
        def step(d, carry):
            act(lax.rem(mine + d, n))
            return carry

        lax.fori_loop(lead, n, step, 0)

    def each_layer(act):
        def step(d, carry):
            act(lax.rem(layer + d, nt))
            return carry

        lax.fori_loop(1, nt, step, 0)

    def is_self(device):
        return jnp.logical_and(device["tm"] == tm_me, device["space"] == me)

    barrier = pltpu.get_barrier_semaphore()

    def greet(device):
        pl.semaphore_signal(barrier, inc=1, device_id=device, device_id_type=MESH)

    def greet_origin(plane):
        origin = {"tm": held, "space": plane}

        @pl.when(jnp.logical_not(is_self(origin)))
        def _():
            greet(origin)

    def greet_target(index):
        target = member_id(home, index)

        @pl.when(jnp.logical_not(is_self(target)))
        def _():
            greet(target)

    each_peer(greet_origin, lead=0)
    each_peer(greet_target, lead=0)
    each_peer(lambda index: greet(member_id(layer, index)))
    each_peer(lambda index: greet({"tm": tm_me, "space": index}), mine=me)
    each_layer(lambda index: greet(member_id(index, member)))

    for k in range(54):
        gauge_own[k] = gauge_ref[k]
    towards = direction_ref[0].astype(jnp.float32)
    gauge_own[54] = jnp.full((1, lanes), towards, jnp.float32)
    plane_at = lax.broadcasted_iota(jnp.int32, (n, lanes), 0).astype(jnp.float32)
    site = lax.broadcasted_iota(jnp.int32, (n, lanes), 1)
    angle = (
        2.0
        * math.pi
        * (
            momentum_ref[0].astype(jnp.float32) * (site % SX).astype(jnp.float32) / SX
            + momentum_ref[1].astype(jnp.float32) * (site // SX).astype(jnp.float32) / SY
            + momentum_ref[2].astype(jnp.float32) * plane_at / n
        )
    )
    table[0] = jnp.cos(angle)
    table[1] = jnp.sin(angle)
    at_home = jnp.where(held == tm_me, 1, 0)
    pl.semaphore_wait(barrier, 2 * (n - at_home) + n - 1 + n - 1 + nt - 1)

    def remote(kind, source, target, device, peer, slot):
        return pltpu.make_async_remote_copy(
            src_ref=source,
            dst_ref=target,
            send_sem=send_sem.at[kind, peer],
            recv_sem=recv_sem.at[kind, slot],
            device_id=device,
            device_id_type=MESH,
        )

    def span_of(piece):
        return pl.ds(pl.multiple_of(piece * chunk, chunk), chunk)

    def gauge_home():
        return remote(1, gauge_own, gauge_all.at[me], member_id(home, me), 0, 0)

    def gauge_copy(peer, slot):
        return remote(
            0, gauge_all.at[slot], gauge_all.at[slot], member_id(layer, peer), peer, slot
        )

    def field_copy(device, peer, slot, piece):
        span = span_of(piece)
        source, target = field_ref.at[:, peer, span], field_in.at[slot, :, span]
        return remote(8 + piece, source, target, device, peer, slot)

    def home_copy(piece):
        span = span_of(piece)
        return pltpu.make_async_copy(
            field_ref.at[:, member, span], field_in.at[me, :, span], local_sem.at[piece]
        )

    def twice_copy(peer, slot, piece):
        span = span_of(piece)
        source, target = twice.at[peer, :, span], twice_in.at[slot, :, span]
        kind = 8 + per_plane + piece
        return remote(kind, source, target, member_id(layer, peer), peer, slot)

    def gradient_copy(peer, slot, piece):
        span = span_of(piece)
        source, target = gradient.at[peer, :, span], gradient_in.at[slot, :, span]
        kind = 8 + 2 * per_plane + piece
        return remote(kind, source, target, member_id(layer, peer), peer, slot)

    def part_copy(peer, slot):
        return remote(4, part_send.at[peer], part_in.at[slot], member_id(layer, peer), peer, slot)

    def sink_copy(device, peer, slot):
        return remote(5, own_send, rows_sink.at[slot], device, peer, slot)

    def source_copy(peer, slot):
        return remote(6, source_send, rows_source.at[slot], member_id(layer, peer), peer, slot)

    def trace_copy(peer, slot):
        return remote(
            7, trace_send, trace_in.at[slot], {"tm": tm_me, "space": peer}, peer, slot
        )

    def start_all(copy, mine=member):
        each_peer(lambda peer: copy(peer, mine).start(), mine=mine)

    def arrive_all(copy, mine=member):
        each_peer(lambda peer: copy(peer, peer).wait_recv(), mine=mine)

    gauge_stays = is_self(member_id(home, me))

    @pl.when(jnp.logical_not(gauge_stays))
    def _():
        gauge_home().start()

    @pl.when(gauge_stays)
    def _():
        gauge_all[me] = gauge_own[...]

    def each_piece(act):
        def step(piece, carry):
            act(piece)
            return carry

        lax.fori_loop(0, per_plane, step, 0)

    def send_fields(piece):
        def send_field(peer):
            device = member_id(home, peer)

            @pl.when(jnp.logical_not(is_self(device)))
            def _():
                field_copy(device, peer, me, piece).start()

        each_peer(send_field, lead=0)

        @pl.when(held == tm_me)
        def _():
            home_copy(piece).start()

    each_piece(send_fields)

    @pl.when(jnp.logical_not(is_self({"tm": held, "space": member})))
    def _():
        gauge_home().wait_recv()

    start_all(gauge_copy)


    def take_field(plane, piece):
        origin = {"tm": held, "space": plane}
        mine = is_self(origin)

        @pl.when(jnp.logical_not(mine))
        def _():
            device = member_id(home, lax.rem(member + 1, n))
            field_copy(device, plane, plane, piece).wait_recv()

        @pl.when(mine)
        def _():
            home_copy(piece).wait()

    arrive_all(gauge_copy)

    def widen(z, carry):
        for k in range(54):
            gauge_wide[z, k] = jnp.broadcast_to(gauge_all[z, k], (8, lanes))
        return carry

    lax.fori_loop(0, n, widen, 0)

    column = lax.broadcasted_iota(jnp.int32, (chunk, lanes), 1) % SX

    def link_at(z, direction):
        def link(part, i, j):
            tile = gauge_wide[z, ((direction * 2 + part) * 3 + i) * 3 + j]
            return jnp.concatenate([tile] * (chunk // 8), axis=0)

        return link

    def sweep(held, out, z, piece):
        span = pl.ds(pl.multiple_of(piece * chunk, chunk), chunk)
        above = lax.rem(z + 1, n)
        below = lax.rem(z + n - 1, n)

        def field_at(plane):
            return [held[plane, k, span, :].astype(jnp.float32) for k in range(6)]

        here = field_at(z)
        total = [-6.0 * part for part in here]

        def add(terms):
            for k in range(6):
                total[k] = total[k] + terms[k]

        add(apply_link(link_at(z, 0), [ahead_x(part, column) for part in here]))
        add([behind_x(part, column) for part in apply_adjoint(link_at(z, 0), here)])
        add(apply_link(link_at(z, 1), [ahead_y(part) for part in here]))
        add([behind_y(part) for part in apply_adjoint(link_at(z, 1), here)])
        add(apply_link(link_at(z, 2), field_at(above)))
        add(rounded(apply_adjoint(link_at(below, 2), field_at(below))))
        for k in range(6):
            out[z, k, span, :] = (here[k] + smear_kappa * total[k]).astype(jnp.bfloat16)

    def derive(z, piece):
        span = pl.ds(pl.multiple_of(piece * chunk, chunk), chunk)
        above = lax.rem(z + 1, n)
        below = lax.rem(z + n - 1, n)

        def field_at(plane):
            return [twice[plane, k, span, :].astype(jnp.float32) for k in range(6)]

        pick = jnp.broadcast_to(gauge_all[z, 54], (chunk, lanes))
        wide_x = pick == 0.0
        wide_y = pick == 1.0
        wide_z = pick == 2.0
        links = [link_at(z, direction) for direction in range(3)]
        link_below = link_at(below, 2)

        def chosen(part, i, j):
            return jnp.where(
                wide_x,
                links[0](part, i, j),
                jnp.where(wide_y, links[1](part, i, j), links[2](part, i, j)),
            )

        def chosen_back(part, i, j):
            return jnp.where(
                wide_x,
                links[0](part, i, j),
                jnp.where(wide_y, links[1](part, i, j), link_below(part, i, j)),
            )

        here = field_at(z)
        up = field_at(above)
        down = field_at(below)
        incoming = [
            jnp.where(
                wide_x, ahead_x(here[k], column), jnp.where(wide_y, ahead_y(here[k]), up[k])
            )
            for k in range(6)
        ]
        base = [jnp.where(wide_z, down[k], here[k]) for k in range(6)]
        forward = apply_link(chosen, incoming)
        back = apply_adjoint(chosen_back, base)
        back = [
            jnp.where(wide_x, behind_x(part, column), jnp.where(wide_y, behind_y(part), carried))
            for part, carried in zip(back, rounded(back))
        ]
        slope = [forward[k] - back[k] for k in range(6)]
        cosine = table[0, pl.ds(z, 1), :]
        sine = table[1, pl.ds(z, 1), :]
        for c in range(3):
            real, imag = slope[c], slope[3 + c]
            gradient[z, c, span, :] = (cosine * real + sine * imag).astype(jnp.bfloat16)
            gradient[z, 3 + c, span, :] = (cosine * imag - sine * real).astype(jnp.bfloat16)

    turn = jnp.where(2 * layer < nt, 1, -1)
    begin = jnp.where(2 * layer < nt, layer * per + 1, layer * per)

    step = 2 if n % 2 == 0 else 1

    def work(piece):
        def first_planes(e, carry):
            group = [lax.rem(begin + turn * (e * step + g) + n, n) for g in range(step)]

            @pl.when(e == 0)
            def _():
                take_field(lax.rem(group[0] - turn + n, n), piece)
                take_field(group[0], piece)

            for g, z in enumerate(group):

                @pl.when(e * step + g < n - 2)
                def _(z=z):
                    take_field(lax.rem(z + turn + n, n), piece)

            for z in group:
                sweep(field_in, once, z, piece)
            return carry

        def last_planes(e, carry):
            group = [lax.rem(member + e * step + g + 1, n) for g in range(step)]
            for z in group:
                sweep(once, twice, z, piece)
            for g, z in enumerate(group):

                @pl.when(e * step + g + 1 < n)
                def _(z=z):
                    twice_copy(z, member, piece).start()

            return carry

        def derive_planes(e, carry):
            group = [lax.rem(member + e * step + g + 1, n) for g in range(step)]
            for z in group:
                derive(z, piece)
            for g, z in enumerate(group):

                @pl.when(e * step + g + 1 < n)
                def _(z=z):
                    gradient_copy(z, member, piece).start()

            return carry

        lax.fori_loop(0, n // step, first_planes, 0)
        lax.fori_loop(0, n // step, last_planes, 0)
        lax.fori_loop(0, n // step, derive_planes, 0)

    each_piece(work)
    twice_in[member] = twice[member]
    gradient_in[member] = gradient[member]

    def arrive_piece(piece):
        each_peer(lambda peer: twice_copy(peer, peer, piece).wait_recv())
        each_peer(lambda peer: gradient_copy(peer, peer, piece).wait_recv())

    each_piece(arrive_piece)
    left = jnp.concatenate([flat_rows(twice_in[:, k]) for k in range(6)], axis=1)
    parts = [flat_rows(gradient_in[:, k]) for k in range(6)]
    right_real = jnp.concatenate(parts, axis=1)
    right_imag = jnp.concatenate(parts[3:] + [-part for part in parts[:3]], axis=1)
    nt_dims = (((1,), (1,)), ((), ()))
    sum_real = lax.dot_general(left, right_real, nt_dims, preferred_element_type=jnp.float32)
    sum_imag = lax.dot_general(left, right_imag, nt_dims, preferred_element_type=jnp.float32)
    part_send[:, :, :nv] = sum_real.reshape(n, rows, nv).astype(jnp.bfloat16)
    part_send[:, :, nv:] = sum_imag.reshape(n, rows, nv).astype(jnp.bfloat16)
    part_in[member] = part_send[member]
    start_all(part_copy)
    arrive_all(part_copy)
    scale = 1.0 / math.sqrt(3 * SX * SY * n)
    summed = jnp.sum(part_in[...].astype(jnp.float32), axis=0)
    own = (summed * scale).astype(jnp.bfloat16)
    own_send[...] = own
    rows_all[held] = own

    def layer_copy(peer, slot):
        return pltpu.make_async_remote_copy(
            src_ref=own_send,
            dst_ref=rows_all.at[slot],
            send_sem=tm_send_sem.at[peer],
            recv_sem=tm_recv_sem.at[slot],
            device_id=member_id(peer, member),
            device_id_type=MESH,
        )

    def send_sink(plane):
        device = {"tm": held, "space": plane}

        @pl.when(jnp.logical_not(is_self(device)))
        def _():
            sink_copy(device, plane, member).start()

    def take_sink(index):
        origin = member_id(home, index)

        @pl.when(jnp.logical_not(is_self(origin)))
        def _():
            sink_copy({"tm": tm_me, "space": lax.rem(me + 1, n)}, index, index).wait_recv()

    each_layer(lambda peer: layer_copy(peer, held).start())
    each_peer(send_sink, mine=me, lead=0)

    @pl.when(held == tm_me)
    def _():
        rows_sink[member] = own_send[...]

    each_layer(lambda peer: layer_copy(peer, slice_of(peer)).wait_recv())
    source_send[...] = rows_all[source_ref[layer]]
    start_all(source_copy)
    rows_source[member] = source_send[...]
    each_peer(take_sink, lead=0)
    load_blocks.wait()

    mine_rows = rows_sink[me].astype(jnp.float32)
    own_ref[:, 0, :] = mine_rows[:, :nv].astype(jnp.bfloat16)
    own_ref[:, 1, :] = mine_rows[:, nv:].astype(jnp.bfloat16)
    sink = flat_rows(rows_sink[...])

    pair = 2 if blocks.shape[0] % 2 == 0 else 1

    def first_block(q):
        real = blocks[q, 0]
        imag = blocks[q, 1]
        tall = jnp.concatenate([real, -imag], axis=0)
        tall_imag = jnp.concatenate([imag, real], axis=0)
        firsts[q, :, :nv] = jnp.dot(sink, tall, preferred_element_type=jnp.float32).astype(
            jnp.bfloat16
        )
        firsts[q, :, nv:] = jnp.dot(sink, tall_imag, preferred_element_type=jnp.float32).astype(
            jnp.bfloat16
        )

    def first_blocks(e, carry):
        for g in range(pair):
            first_block(e * pair + g)
        return carry

    lax.fori_loop(0, blocks.shape[0] // pair, first_blocks, 0)
    arrive_all(source_copy)
    partner = flat_rows(rows_source[...])
    partner_real, partner_imag = partner[:, :nv], partner[:, nv:]
    right_side[:nv, :nv] = partner_real
    right_side[:nv, nv:] = partner_imag
    right_side[nv:, :nv] = -partner_imag
    right_side[nv:, nv:] = partner_real

    def fold(values):
        return jnp.sum(values.reshape(nv // 8, 8, nv), axis=0)

    def second_block(q, sum_real, sum_imag):
        second = jnp.dot(firsts[q], right_side[...], preferred_element_type=jnp.float32)
        second_real, second_imag = second[:, :nv], second[:, nv:]
        real = blocks[q, 0].astype(jnp.float32)
        imag = blocks[q, 1].astype(jnp.float32)
        sum_real = sum_real + fold(second_real * real + second_imag * imag)
        sum_imag = sum_imag + fold(second_imag * real - second_real * imag)
        return sum_real, sum_imag

    def second_blocks(e, carry):
        for g in range(pair):
            carry = second_block(e * pair + g, *carry)
        return carry

    nothing = jnp.zeros((8, nv), jnp.float32)
    sum_real, sum_imag = lax.fori_loop(
        0, blocks.shape[0] // pair, second_blocks, (nothing, nothing)
    )
    trace_real = jnp.sum(sum_real)
    trace_imag = jnp.sum(sum_imag)
    row = lax.broadcasted_iota(jnp.int32, trace_send.shape, 0)
    lane = lax.broadcasted_iota(jnp.int32, trace_send.shape, 1)
    mine = source_ref[layer]
    value = jnp.where(row == 0, trace_real, jnp.where(row == 1, trace_imag, 0.0))
    value = jnp.where(lane == mine, value, 0.0) * (1.0 / (NS * nv))
    trace_send[...] = value
    trace_in[me] = value
    start_all(trace_copy, mine=me)
    arrive_all(trace_copy, mine=me)
    total = jnp.sum(trace_in[...], axis=0)
    trace_ref[0] = total[0:1, :nt]
    trace_ref[1] = total[1:2, :nt]

    @pl.when(jnp.logical_not(gauge_stays))
    def _():
        gauge_home().wait_send()

    def sent_piece(piece):
        def sent_field(peer):
            device = member_id(home, peer)

            @pl.when(jnp.logical_not(is_self(device)))
            def _():
                field_copy(device, peer, me, piece).wait_send()

        each_peer(sent_field, lead=0)
        each_peer(lambda peer: twice_copy(peer, member, piece).wait_send())
        each_peer(lambda peer: gradient_copy(peer, member, piece).wait_send())

    each_piece(sent_piece)

    def sent_sink(plane):
        device = {"tm": held, "space": plane}

        @pl.when(jnp.logical_not(is_self(device)))
        def _():
            sink_copy(device, plane, member).wait_send()

    each_peer(sent_sink, mine=me, lead=0)
    for copy in (gauge_copy, part_copy, source_copy):
        each_peer(lambda peer: copy(peer, member).wait_send())
    each_peer(lambda peer: trace_copy(peer, me).wait_send(), mine=me)
    each_layer(lambda peer: layer_copy(peer, held).wait_send())


def per_device(n, nt, vectors, gauge_links, perambulator, directions, momentum, source_list):
    nv = vectors.shape[4]
    lanes = vectors.shape[5]
    rows = nv // n
    field = vectors.reshape(6, n, rows, lanes)
    gauge = gauge_links.reshape(54, 1, lanes)
    block_set = perambulator[0]

    bf16, f32 = jnp.bfloat16, jnp.float32
    vmem = pl.BlockSpec(memory_space=pltpu.VMEM)
    smem = pl.BlockSpec(memory_space=pltpu.SMEM)
    anywhere = pl.BlockSpec(memory_space=pltpu.HBM)
    split = (n, 6, rows, lanes)
    count = block_set.shape[0]
    pieces = rows // row_chunk(rows)
    own, trace = pl.pallas_call(
        lambda *refs: kernel(n, nt, *refs),
        out_shape=(
            jax.ShapeDtypeStruct((rows, 2, nv), bf16),
            jax.ShapeDtypeStruct((2, 1, nt), f32),
        ),
        in_specs=[smem, smem, smem, anywhere, vmem, anywhere],
        out_specs=(vmem, vmem),
        scratch_shapes=[
            pltpu.VMEM((55, 1, lanes), f32),
            pltpu.VMEM((n, 55, 1, lanes), f32),
            pltpu.VMEM((n, 54, 8, lanes), f32),
            pltpu.VMEM((2, n, lanes), f32),
            pltpu.VMEM(split, bf16),
            pltpu.VMEM(split, bf16),
            pltpu.VMEM(split, bf16),
            pltpu.VMEM(split, bf16),
            pltpu.VMEM(split, bf16),
            pltpu.VMEM(split, bf16),
            pltpu.VMEM((n, rows, 2 * nv), bf16),
            pltpu.VMEM((n, rows, 2 * nv), bf16),
            pltpu.VMEM((rows, 2 * nv), bf16),
            pltpu.VMEM((nt, rows, 2 * nv), bf16),
            pltpu.VMEM((n, rows, 2 * nv), bf16),
            pltpu.VMEM((rows, 2 * nv), bf16),
            pltpu.VMEM((n, rows, 2 * nv), bf16),
            pltpu.VMEM((count, 2, nv, nv), bf16),
            pltpu.VMEM((count, nv, 2 * nv), bf16),
            pltpu.VMEM((2 * nv, 2 * nv), bf16),
            pltpu.VMEM((8, 128), f32),
            pltpu.VMEM((n, 8, 128), f32),
            pltpu.SemaphoreType.DMA((8 + 3 * pieces, n)),
            pltpu.SemaphoreType.DMA((8 + 3 * pieces, n)),
            pltpu.SemaphoreType.DMA((nt,)),
            pltpu.SemaphoreType.DMA((nt,)),
            pltpu.SemaphoreType.DMA,
            pltpu.SemaphoreType.DMA((pieces,)),
        ],
        compiler_params=pltpu.CompilerParams(
            collective_id=0, has_side_effects=True, vmem_limit_bytes=60 * 1024 * 1024
        ),
        name="meson",
    )(source_list, directions, momentum, field, gauge, block_set)
    return (own[None], trace)


def solution(mesh):
    in_specs = (
        P("tm", None, "space", None, None, None),
        P("tm", None, None, "space", None, None, None),
        P("tm", "space", None, None, None),
        P("tm"),
        P(),
        P(),
    )
    out_specs = (P("tm", "space", None, None), P(None, "tm", None))
    n, nt = mesh.shape["space"], mesh.shape["tm"]

    def body(*args):
        return per_device(n, nt, *args)

    return jax.shard_map(
        body, mesh=mesh, in_specs=in_specs, out_specs=out_specs, check_vma=False
    )
```

```python
import math

import jax
import jax.numpy as jnp
from jax import lax
from jax.experimental import pallas as pl
from jax.experimental.pallas import tpu as pltpu
from jax.sharding import PartitionSpec as P

NS = 4
SX = 16
SY = 8
SMEAR = 2

MESH = pl.DeviceIdType.MESH
smear_kappa = 0.05


def row_chunk(rows):
    return 16 if rows % 16 == 0 else rows


def flat_rows(block):
    count, rows, lanes = block.shape
    if rows % 16 == 0:
        return block.reshape(count * rows, lanes)
    wide = block.astype(jnp.float32).reshape(count * rows, lanes)
    return wide.astype(jnp.bfloat16)


def apply_link(link, field):
    real = []
    imag = []
    for i in range(3):
        total_real = None
        total_imag = None
        for j in range(3):
            link_real, link_imag = link(0, i, j), link(1, i, j)
            term_real = link_real * field[j] - link_imag * field[3 + j]
            term_imag = link_real * field[3 + j] + link_imag * field[j]
            total_real = term_real if j == 0 else total_real + term_real
            total_imag = term_imag if j == 0 else total_imag + term_imag
        real.append(total_real)
        imag.append(total_imag)
    return real + imag


def rounded(field):
    return [part.astype(jnp.bfloat16).astype(jnp.float32) for part in field]


def apply_adjoint(link, field):
    real = []
    imag = []
    for i in range(3):
        total_real = None
        total_imag = None
        for j in range(3):
            link_real, link_imag = link(0, j, i), link(1, j, i)
            term_real = link_real * field[j] + link_imag * field[3 + j]
            term_imag = link_real * field[3 + j] - link_imag * field[j]
            total_real = term_real if j == 0 else total_real + term_real
            total_imag = term_imag if j == 0 else total_imag + term_imag
        real.append(total_real)
        imag.append(total_imag)
    return real + imag


def ahead_x(part, column):
    return jnp.where(column == SX - 1, pltpu.roll(part, SX - 1, 1), pltpu.roll(part, SX * SY - 1, 1))


def behind_x(part, column):
    return jnp.where(column == 0, pltpu.roll(part, SX * SY - SX + 1, 1), pltpu.roll(part, 1, 1))


def ahead_y(part):
    return pltpu.roll(part, SX * SY - SX, 1)


def behind_y(part):
    return pltpu.roll(part, SX, 1)


def kernel(
    n,
    nt,
    source_ref,
    direction_ref,
    momentum_ref,
    field_ref,
    gauge_ref,
    block_ref,
    own_ref,
    trace_ref,
    gauge_own,
    gauge_all,
    gauge_wide,
    table,
    field_in,
    once,
    twice,
    gradient,
    twice_in,
    gradient_in,
    part_send,
    part_in,
    own_send,
    rows_all,
    rows_sink,
    source_send,
    rows_source,
    blocks,
    firsts,
    right_side,
    trace_send,
    trace_in,
    send_sem,
    recv_sem,
    tm_send_sem,
    tm_recv_sem,
    block_sem,
    local_sem,
):
    me = lax.axis_index("space")
    tm_me = lax.axis_index("tm")
    per = n // nt
    layer = me // per
    member = tm_me * per + lax.rem(me, per)
    half = max(nt // 2, 1)

    def layer_of(timeslice):
        return lax.rem(timeslice, 2) * half + timeslice // 2

    def slice_of(index):
        return lax.rem(index, half) * 2 + index // half

    home = layer_of(tm_me)
    held = slice_of(layer)
    per_plane, chunk = field_ref.shape[1], field_ref.shape[3]
    rows = per_plane * chunk
    width = n * chunk
    lanes = SX * SY
    nv = n * rows

    load_blocks = pltpu.make_async_copy(block_ref, blocks, block_sem)
    load_blocks.start()

    def member_id(which, index):
        return {"tm": index // per, "space": which * per + lax.rem(index, per)}

    def each_peer(act, mine=member, lead=1):
        def step(d, carry):
            act(lax.rem(mine + d, n))
            return carry

        lax.fori_loop(lead, n, step, 0)

    def each_layer(act):
        def step(d, carry):
            act(lax.rem(layer + d, nt))
            return carry

        lax.fori_loop(1, nt, step, 0)

    def is_self(device):
        return jnp.logical_and(device["tm"] == tm_me, device["space"] == me)

    barrier = pltpu.get_barrier_semaphore()

    def greet(device):
        pl.semaphore_signal(barrier, inc=1, device_id=device, device_id_type=MESH)

    def greet_origin(plane):
        origin = {"tm": held, "space": plane}

        @pl.when(jnp.logical_not(is_self(origin)))
        def _():
            greet(origin)

    def greet_target(index):
        target = member_id(home, index)

        @pl.when(jnp.logical_not(is_self(target)))
        def _():
            greet(target)

    each_peer(greet_origin, lead=0)
    each_peer(greet_target, lead=0)
    each_peer(lambda index: greet(member_id(layer, index)))
    each_peer(lambda index: greet({"tm": tm_me, "space": index}), mine=me)
    each_layer(lambda index: greet(member_id(index, member)))

    for k in range(54):
        gauge_own[k] = gauge_ref[k]
    towards = direction_ref[0].astype(jnp.float32)
    gauge_own[54] = jnp.full((1, lanes), towards, jnp.float32)
    plane_at = lax.broadcasted_iota(jnp.int32, (n, lanes), 0).astype(jnp.float32)
    site = lax.broadcasted_iota(jnp.int32, (n, lanes), 1)
    angle = (
        2.0
        * math.pi
        * (
            momentum_ref[0].astype(jnp.float32) * (site % SX).astype(jnp.float32) / SX
            + momentum_ref[1].astype(jnp.float32) * (site // SX).astype(jnp.float32) / SY
            + momentum_ref[2].astype(jnp.float32) * plane_at / n
        )
    )
    table[0] = jnp.cos(angle)
    table[1] = jnp.sin(angle)
    at_home = jnp.where(held == tm_me, 1, 0)
    pl.semaphore_wait(barrier, 2 * (n - at_home) + n - 1 + n - 1 + nt - 1)

    def remote(kind, source, target, device, peer, slot):
        return pltpu.make_async_remote_copy(
            src_ref=source,
            dst_ref=target,
            send_sem=send_sem.at[kind, peer],
            recv_sem=recv_sem.at[kind, slot],
            device_id=device,
            device_id_type=MESH,
        )

    def span_of(piece):
        return pl.ds(pl.multiple_of(piece * chunk, chunk), chunk)

    def gauge_home():
        return remote(1, gauge_own, gauge_all.at[me], member_id(home, me), 0, 0)

    def gauge_copy(peer, slot):
        return remote(
            0, gauge_all.at[slot], gauge_all.at[slot], member_id(layer, peer), peer, slot
        )

    def field_copy(device, peer, slot, piece):
        span = span_of(piece)
        source, target = field_ref.at[:, piece, peer], field_in.at[slot, :, span]
        return remote(8 + piece, source, target, device, peer, slot)

    def home_copy(piece):
        span = span_of(piece)
        return pltpu.make_async_copy(
            field_ref.at[:, piece, member], field_in.at[me, :, span], local_sem.at[piece]
        )

    def twice_copy(peer, slot, piece):
        span = span_of(piece)
        source, target = twice.at[peer, :, span], twice_in.at[slot, :, span]
        kind = 8 + per_plane + piece
        return remote(kind, source, target, member_id(layer, peer), peer, slot)

    def gradient_copy(peer, slot, piece):
        span = span_of(piece)
        source, target = gradient.at[peer, :, span], gradient_in.at[slot, :, span]
        kind = 8 + 2 * per_plane + piece
        return remote(kind, source, target, member_id(layer, peer), peer, slot)

    def part_copy(peer, slot, piece):
        source, target = part_send.at[piece, peer], part_in.at[piece, slot]
        kind = 8 + 3 * per_plane + piece
        return remote(kind, source, target, member_id(layer, peer), peer, slot)

    def sink_copy(device, peer, slot, piece):
        kind = 8 + 4 * per_plane + piece
        return remote(
            kind, own_send.at[piece], rows_sink.at[piece, slot], device, peer, slot
        )

    def source_copy(peer, slot):
        return remote(6, source_send, rows_source.at[slot], member_id(layer, peer), peer, slot)

    def trace_copy(peer, slot):
        return remote(
            7, trace_send, trace_in.at[slot], {"tm": tm_me, "space": peer}, peer, slot
        )

    def start_all(copy, mine=member):
        each_peer(lambda peer: copy(peer, mine).start(), mine=mine)

    def arrive_all(copy, mine=member):
        each_peer(lambda peer: copy(peer, peer).wait_recv(), mine=mine)

    gauge_stays = is_self(member_id(home, me))

    @pl.when(jnp.logical_not(gauge_stays))
    def _():
        gauge_home().start()

    @pl.when(gauge_stays)
    def _():
        gauge_all[me] = gauge_own[...]

    def each_piece(act):
        def step(piece, carry):
            act(piece)
            return carry

        lax.fori_loop(0, per_plane, step, 0)

    def send_fields(piece):
        def send_field(peer):
            device = member_id(home, peer)

            @pl.when(jnp.logical_not(is_self(device)))
            def _():
                field_copy(device, peer, me, piece).start()

        each_peer(send_field, lead=0)

        @pl.when(held == tm_me)
        def _():
            home_copy(piece).start()

    each_piece(send_fields)

    @pl.when(jnp.logical_not(is_self({"tm": held, "space": member})))
    def _():
        gauge_home().wait_recv()

    start_all(gauge_copy)


    def take_field(plane, piece):
        origin = {"tm": held, "space": plane}
        mine = is_self(origin)

        @pl.when(jnp.logical_not(mine))
        def _():
            device = member_id(home, lax.rem(member + 1, n))
            field_copy(device, plane, plane, piece).wait_recv()

        @pl.when(mine)
        def _():
            home_copy(piece).wait()

    arrive_all(gauge_copy)

    def widen(z, carry):
        for k in range(54):
            gauge_wide[z, k] = jnp.broadcast_to(gauge_all[z, k], (8, lanes))
        return carry

    lax.fori_loop(0, n, widen, 0)

    column = lax.broadcasted_iota(jnp.int32, (chunk, lanes), 1) % SX

    def link_at(z, direction):
        def link(part, i, j):
            tile = gauge_wide[z, ((direction * 2 + part) * 3 + i) * 3 + j]
            return jnp.concatenate([tile] * (chunk // 8), axis=0)

        return link

    def sweep(held, out, z, piece):
        span = pl.ds(pl.multiple_of(piece * chunk, chunk), chunk)
        above = lax.rem(z + 1, n)
        below = lax.rem(z + n - 1, n)

        def field_at(plane):
            return [held[plane, k, span, :].astype(jnp.float32) for k in range(6)]

        here = field_at(z)
        total = [-6.0 * part for part in here]

        def add(terms):
            for k in range(6):
                total[k] = total[k] + terms[k]

        add(apply_link(link_at(z, 0), [ahead_x(part, column) for part in here]))
        add([behind_x(part, column) for part in apply_adjoint(link_at(z, 0), here)])
        add(apply_link(link_at(z, 1), [ahead_y(part) for part in here]))
        add([behind_y(part) for part in apply_adjoint(link_at(z, 1), here)])
        add(apply_link(link_at(z, 2), field_at(above)))
        add(rounded(apply_adjoint(link_at(below, 2), field_at(below))))
        for k in range(6):
            out[z, k, span, :] = (here[k] + smear_kappa * total[k]).astype(jnp.bfloat16)

    def derive(z, piece):
        span = pl.ds(pl.multiple_of(piece * chunk, chunk), chunk)
        above = lax.rem(z + 1, n)
        below = lax.rem(z + n - 1, n)

        def field_at(plane):
            return [twice[plane, k, span, :].astype(jnp.float32) for k in range(6)]

        pick = jnp.broadcast_to(gauge_all[z, 54], (chunk, lanes))
        wide_x = pick == 0.0
        wide_y = pick == 1.0
        wide_z = pick == 2.0
        links = [link_at(z, direction) for direction in range(3)]
        link_below = link_at(below, 2)

        def chosen(part, i, j):
            return jnp.where(
                wide_x,
                links[0](part, i, j),
                jnp.where(wide_y, links[1](part, i, j), links[2](part, i, j)),
            )

        def chosen_back(part, i, j):
            return jnp.where(
                wide_x,
                links[0](part, i, j),
                jnp.where(wide_y, links[1](part, i, j), link_below(part, i, j)),
            )

        here = field_at(z)
        up = field_at(above)
        down = field_at(below)
        incoming = [
            jnp.where(
                wide_x, ahead_x(here[k], column), jnp.where(wide_y, ahead_y(here[k]), up[k])
            )
            for k in range(6)
        ]
        base = [jnp.where(wide_z, down[k], here[k]) for k in range(6)]
        forward = apply_link(chosen, incoming)
        back = apply_adjoint(chosen_back, base)
        back = [
            jnp.where(wide_x, behind_x(part, column), jnp.where(wide_y, behind_y(part), carried))
            for part, carried in zip(back, rounded(back))
        ]
        slope = [forward[k] - back[k] for k in range(6)]
        cosine = table[0, pl.ds(z, 1), :]
        sine = table[1, pl.ds(z, 1), :]
        for c in range(3):
            real, imag = slope[c], slope[3 + c]
            gradient[z, c, span, :] = (cosine * real + sine * imag).astype(jnp.bfloat16)
            gradient[z, 3 + c, span, :] = (cosine * imag - sine * real).astype(jnp.bfloat16)

    turn = jnp.where(2 * layer < nt, 1, -1)
    begin = jnp.where(2 * layer < nt, layer * per + 1, layer * per)

    step = 2 if n % 2 == 0 else 1

    def work(piece):
        def first_planes(e, carry):
            group = [lax.rem(begin + turn * (e * step + g) + n, n) for g in range(step)]

            @pl.when(e == 0)
            def _():
                take_field(lax.rem(group[0] - turn + n, n), piece)
                take_field(group[0], piece)

            for g, z in enumerate(group):

                @pl.when(e * step + g < n - 2)
                def _(z=z):
                    take_field(lax.rem(z + turn + n, n), piece)

            for z in group:
                sweep(field_in, once, z, piece)
            return carry

        def last_planes(e, carry):
            group = [lax.rem(member + e * step + g + 1, n) for g in range(step)]
            for z in group:
                sweep(once, twice, z, piece)
            for g, z in enumerate(group):

                @pl.when(e * step + g + 1 < n)
                def _(z=z):
                    twice_copy(z, member, piece).start()

            return carry

        def derive_planes(e, carry):
            group = [lax.rem(member + e * step + g + 1, n) for g in range(step)]
            for z in group:
                derive(z, piece)
            for g, z in enumerate(group):

                @pl.when(e * step + g + 1 < n)
                def _(z=z):
                    gradient_copy(z, member, piece).start()

            return carry

        lax.fori_loop(0, n // step, first_planes, 0)
        lax.fori_loop(0, n // step, last_planes, 0)
        lax.fori_loop(0, n // step, derive_planes, 0)

    each_piece(work)
    twice_in[member] = twice[member]
    gradient_in[member] = gradient[member]

    def piece_rows(held_ref, k, piece):
        return flat_rows(held_ref[:, k, piece * chunk : (piece + 1) * chunk, :])

    for piece in range(per_plane):
        each_peer(lambda peer: twice_copy(peer, peer, piece).wait_recv())
    left = jnp.concatenate(
        [
            jnp.concatenate([piece_rows(twice_in, k, piece) for k in range(6)], axis=1)
            for piece in range(per_plane)
        ],
        axis=0,
    )
    nt_dims = (((1,), (1,)), ((), ()))
    for piece in range(per_plane):
        each_peer(lambda peer: gradient_copy(peer, peer, piece).wait_recv())
        parts = [piece_rows(gradient_in, k, piece) for k in range(6)]
        right_real = jnp.concatenate(parts, axis=1)
        right_imag = jnp.concatenate(parts[3:] + [-part for part in parts[:3]], axis=1)
        right = jnp.concatenate([right_real, right_imag], axis=0)
        part = lax.dot_general(left, right, nt_dims, preferred_element_type=jnp.float32)
        part_send[piece] = part.reshape(n, rows, 2 * width).astype(jnp.bfloat16)
        part_in[piece, member] = part_send[piece, member]
        each_peer(lambda peer: part_copy(peer, member, piece).start())

    def layer_copy(peer, slot, piece):
        return pltpu.make_async_remote_copy(
            src_ref=own_send.at[piece],
            dst_ref=rows_all.at[piece, slot],
            send_sem=tm_send_sem.at[piece, peer],
            recv_sem=tm_recv_sem.at[piece, slot],
            device_id=member_id(peer, member),
            device_id_type=MESH,
        )

    scale = 1.0 / math.sqrt(3 * SX * SY * n)
    for piece in range(per_plane):
        each_peer(lambda peer: part_copy(peer, peer, piece).wait_recv())
        summed = jnp.sum(part_in[piece].astype(jnp.float32), axis=0)
        own = (summed * scale).astype(jnp.bfloat16)
        own_send[piece] = own
        rows_all[piece, held] = own

        def send_sink(plane):
            device = {"tm": held, "space": plane}

            @pl.when(jnp.logical_not(is_self(device)))
            def _():
                sink_copy(device, plane, member, piece).start()

        each_layer(lambda peer: layer_copy(peer, held, piece).start())
        each_peer(send_sink, mine=me, lead=0)

        @pl.when(held == tm_me)
        def _():
            rows_sink[piece, member] = own_send[piece]

    def take_sink(index, piece):
        origin = member_id(home, index)

        @pl.when(jnp.logical_not(is_self(origin)))
        def _():
            device = {"tm": tm_me, "space": lax.rem(me + 1, n)}
            sink_copy(device, index, index, piece).wait_recv()

    for piece in range(per_plane):
        each_layer(lambda peer: layer_copy(peer, slice_of(peer), piece).wait_recv())
    for piece in range(per_plane):
        source_send[piece] = rows_all[piece, source_ref[layer]]
    start_all(source_copy)
    rows_source[member] = source_send[...]

    def whole_rows(halves):
        real = [part[:, :width] for part in halves]
        imag = [part[:, width:] for part in halves]
        return jnp.concatenate(real, axis=1), jnp.concatenate(imag, axis=1)

    for piece in range(per_plane):
        each_peer(lambda index: take_sink(index, piece), lead=0)
    load_blocks.wait()

    mine_real, mine_imag = whole_rows(
        [rows_sink[piece, me].astype(jnp.float32) for piece in range(per_plane)]
    )
    own_ref[:, 0, :] = mine_real.astype(jnp.bfloat16)
    own_ref[:, 1, :] = mine_imag.astype(jnp.bfloat16)
    sink = jnp.concatenate(
        whole_rows([flat_rows(rows_sink[piece]) for piece in range(per_plane)]), axis=1
    )

    pair = 2 if blocks.shape[0] % 2 == 0 else 1

    def first_block(q):
        real = blocks[q, 0]
        imag = blocks[q, 1]
        tall = jnp.concatenate([real, -imag], axis=0)
        tall_imag = jnp.concatenate([imag, real], axis=0)
        firsts[q, :, :nv] = jnp.dot(sink, tall, preferred_element_type=jnp.float32).astype(
            jnp.bfloat16
        )
        firsts[q, :, nv:] = jnp.dot(sink, tall_imag, preferred_element_type=jnp.float32).astype(
            jnp.bfloat16
        )

    def first_blocks(e, carry):
        for g in range(pair):
            first_block(e * pair + g)
        return carry

    lax.fori_loop(0, blocks.shape[0] // pair, first_blocks, 0)
    arrive_all(source_copy)
    partner_real, partner_imag = whole_rows(
        [flat_rows(rows_source[:, piece]) for piece in range(per_plane)]
    )
    right_side[:nv, :nv] = partner_real
    right_side[:nv, nv:] = partner_imag
    right_side[nv:, :nv] = -partner_imag
    right_side[nv:, nv:] = partner_real

    def fold(values):
        return jnp.sum(values.reshape(nv // 8, 8, nv), axis=0)

    def second_block(q, sum_real, sum_imag):
        second = jnp.dot(firsts[q], right_side[...], preferred_element_type=jnp.float32)
        second_real, second_imag = second[:, :nv], second[:, nv:]
        real = blocks[q, 0].astype(jnp.float32)
        imag = blocks[q, 1].astype(jnp.float32)
        sum_real = sum_real + fold(second_real * real + second_imag * imag)
        sum_imag = sum_imag + fold(second_imag * real - second_real * imag)
        return sum_real, sum_imag

    def second_blocks(e, carry):
        for g in range(pair):
            carry = second_block(e * pair + g, *carry)
        return carry

    nothing = jnp.zeros((8, nv), jnp.float32)
    sum_real, sum_imag = lax.fori_loop(
        0, blocks.shape[0] // pair, second_blocks, (nothing, nothing)
    )
    trace_real = jnp.sum(sum_real)
    trace_imag = jnp.sum(sum_imag)
    row = lax.broadcasted_iota(jnp.int32, trace_send.shape, 0)
    lane = lax.broadcasted_iota(jnp.int32, trace_send.shape, 1)
    mine = source_ref[layer]
    value = jnp.where(row == 0, trace_real, jnp.where(row == 1, trace_imag, 0.0))
    value = jnp.where(lane == mine, value, 0.0) * (1.0 / (NS * nv))
    trace_send[...] = value
    trace_in[me] = value
    start_all(trace_copy, mine=me)
    arrive_all(trace_copy, mine=me)
    total = jnp.sum(trace_in[...], axis=0)
    trace_ref[0] = total[0:1, :nt]
    trace_ref[1] = total[1:2, :nt]

    @pl.when(jnp.logical_not(gauge_stays))
    def _():
        gauge_home().wait_send()

    def sent_piece(piece):
        def sent_field(peer):
            device = member_id(home, peer)

            @pl.when(jnp.logical_not(is_self(device)))
            def _():
                field_copy(device, peer, me, piece).wait_send()

        each_peer(sent_field, lead=0)
        each_peer(lambda peer: twice_copy(peer, member, piece).wait_send())
        each_peer(lambda peer: gradient_copy(peer, member, piece).wait_send())

    each_piece(sent_piece)

    def sent_sink(plane):
        device = {"tm": held, "space": plane}

        @pl.when(jnp.logical_not(is_self(device)))
        def _():
            for piece in range(per_plane):
                sink_copy(device, plane, member, piece).wait_send()

    each_peer(sent_sink, mine=me, lead=0)
    for copy in (gauge_copy, source_copy):
        each_peer(lambda peer: copy(peer, member).wait_send())
    each_peer(lambda peer: trace_copy(peer, me).wait_send(), mine=me)
    for piece in range(per_plane):
        each_peer(lambda peer: part_copy(peer, member, piece).wait_send())
        each_layer(lambda peer: layer_copy(peer, held, piece).wait_send())


def per_device(n, nt, vectors, gauge_links, perambulator, directions, momentum, source_list):
    nv = vectors.shape[4]
    lanes = vectors.shape[5]
    rows = nv // n
    chunk = row_chunk(rows)
    pieces = rows // chunk
    width = n * chunk
    field = vectors.reshape(6, pieces, n, chunk, lanes)
    gauge = gauge_links.reshape(54, 1, lanes)
    block_set = perambulator[0]

    bf16, f32 = jnp.bfloat16, jnp.float32
    vmem = pl.BlockSpec(memory_space=pltpu.VMEM)
    smem = pl.BlockSpec(memory_space=pltpu.SMEM)
    anywhere = pl.BlockSpec(memory_space=pltpu.HBM)
    split = (n, 6, rows, lanes)
    count = block_set.shape[0]
    own, trace = pl.pallas_call(
        lambda *refs: kernel(n, nt, *refs),
        out_shape=(
            jax.ShapeDtypeStruct((rows, 2, nv), bf16),
            jax.ShapeDtypeStruct((2, 1, nt), f32),
        ),
        in_specs=[smem, smem, smem, anywhere, vmem, anywhere],
        out_specs=(vmem, vmem),
        scratch_shapes=[
            pltpu.VMEM((55, 1, lanes), f32),
            pltpu.VMEM((n, 55, 1, lanes), f32),
            pltpu.VMEM((n, 54, 8, lanes), f32),
            pltpu.VMEM((2, n, lanes), f32),
            pltpu.VMEM(split, bf16),
            pltpu.VMEM(split, bf16),
            pltpu.VMEM(split, bf16),
            pltpu.VMEM(split, bf16),
            pltpu.VMEM(split, bf16),
            pltpu.VMEM(split, bf16),
            pltpu.VMEM((pieces, n, rows, 2 * width), bf16),
            pltpu.VMEM((pieces, n, rows, 2 * width), bf16),
            pltpu.VMEM((pieces, rows, 2 * width), bf16),
            pltpu.VMEM((pieces, nt, rows, 2 * width), bf16),
            pltpu.VMEM((pieces, n, rows, 2 * width), bf16),
            pltpu.VMEM((pieces, rows, 2 * width), bf16),
            pltpu.VMEM((n, pieces, rows, 2 * width), bf16),
            pltpu.VMEM((count, 2, nv, nv), bf16),
            pltpu.VMEM((count, nv, 2 * nv), bf16),
            pltpu.VMEM((2 * nv, 2 * nv), bf16),
            pltpu.VMEM((8, 128), f32),
            pltpu.VMEM((n, 8, 128), f32),
            pltpu.SemaphoreType.DMA((8 + 5 * pieces, n)),
            pltpu.SemaphoreType.DMA((8 + 5 * pieces, n)),
            pltpu.SemaphoreType.DMA((pieces, nt)),
            pltpu.SemaphoreType.DMA((pieces, nt)),
            pltpu.SemaphoreType.DMA,
            pltpu.SemaphoreType.DMA((pieces,)),
        ],
        compiler_params=pltpu.CompilerParams(
            collective_id=0, has_side_effects=True, vmem_limit_bytes=60 * 1024 * 1024
        ),
        name="meson",
    )(source_list, directions, momentum, field, gauge, block_set)
    return (own[None], trace)


def solution(mesh):
    in_specs = (
        P("tm", None, "space", None, None, None),
        P("tm", None, None, "space", None, None, None),
        P("tm", "space", None, None, None),
        P("tm"),
        P(),
        P(),
    )
    out_specs = (P("tm", "space", None, None), P(None, "tm", None))
    n, nt = mesh.shape["space"], mesh.shape["tm"]

    def body(*args):
        return per_device(n, nt, *args)

    return jax.shard_map(
        body, mesh=mesh, in_specs=in_specs, out_specs=out_specs, check_vma=False
    )
```
